128 devices in a mesh: row: 8 (over z, core), col: 16 (over x, y).
Axes of the slice: x: 4, y: 4, z: 4, core: 2. Of those that a mesh axis runs over, the one named last changes fastest.
Arguments:
- object_slices: float32 [2, 2, 4096, 4096], P(None, None, 'row', 'col'), may hold values from -6 to 6
- probe: bfloat16 [4, 2, 256, 256], replicated, may hold values from -6 to 6
- measured: float32 [768, 256, 256], P(('row', 'col')), may hold values from 0 to 3
- tap_row: float32 [2, 64], replicated, may hold values from -0.5 to 0.5
- tap_col: float32 [2, 64], replicated, may hold values from -0.5 to 0.5
- scan_corner: int32 [768, 2], P(('row', 'col')), may hold values from 0 to 3840, as said below
- correlation: int32 [768, 2], P(('row', 'col')), may hold values from 0 to 15, as said below
- scan_count: int32 [8, 16], P('row', 'col'), may hold values from 1 to 6, as said below
Outputs:
- object_grad: float32 [2, 2, 4096, 4096], P(None, None, 'row', 'col')
- probe_grad: float32 [4, 2, 256, 256], replicated
The draws below stay inside these ranges and needn't reach their ends.
Inputs may be any that keep to these rules, and one draw needn't show every extreme that they name: `scan_corner`: the scans of the device at mesh row r start at pixel row r * 512 + a * 128 with a one of 0, 1, 2, and at a pixel column that is a multiple of 128; the left half of the patch lies in tile column correlation[n, 0] and the right half in correlation[n, 1]. correlation[n, 1] equals correlation[n, 0] or is one more. From one device at most 2 patch halves fall in one tile column; in every draw each mesh row has a tile column that receives 2 halves from every device of that row. `scan_count`: slots of a device below its count are live; some device has all 6 live.
All inputs are finite; a program needn't handle non-finite values.
Results may differ from the reference program's by a relative error of at most 0.009.
The reference program's roundings to bfloat16 on the way count: a program that leaves them out, or rounds other values in their place, can miss the bound.
Values may be sent and summed in bfloat16 or wider, within the bound.
No kernel may reach another device: no remote copies, remote signals or barrier semaphores. Data moves between devices by JAX's collectives and lax.ppermute only.
A program may use at most 128 MiB of HBM per device.

```python
import math
import jax
import jax.numpy as jnp
from jax import lax

P_SIZE = 256
M = 4
S = 2
TAPS = 64
SCAN_DEV = 6
HALF = 128
TH = 512
TW = 256
NH = 4096
NW = 4096
SCANS = 768
N_ROW = 8
N_COL = 16


def scan_plan(key):
    tile_key, device_key = jax.random.split(key, 2)
    devices = N_ROW * N_COL
    special = jax.random.randint(tile_key, (N_ROW,), 0, N_COL - 2)
    device_special = jnp.repeat(special, N_COL)
    tile_all = jnp.arange(N_COL, dtype=jnp.int32)

    def one_device(dev_key, chosen):
        key_list = jax.random.split(dev_key, 4)
        ranking = jax.random.permutation(key_list[0], N_COL)
        scores = jnp.where(tile_all == chosen, -2, jnp.where(tile_all == chosen + 1, -1, jnp.where(tile_all == chosen + 2, N_COL + 5, ranking)))
        tile_ids = jnp.argsort(scores, stable=True)[:SCAN_DEV].astype(jnp.int32)
        occupied = jnp.zeros((N_COL,), jnp.int32).at[tile_ids].set(1)
        flip_draw = jax.random.randint(key_list[1], (N_COL,), 0, 2)

        def step(next_free, column):
            here = occupied[column] == 1
            wanted = (column == chosen + 1) | (column != chosen) & (flip_draw[column] == 1)
            flipped = here & (column < N_COL - 1) & next_free & wanted
            return (~here | flipped, flipped.astype(jnp.int32))
        unused, flips = lax.scan(step, jnp.bool_(True), tile_all, reverse=True)
        flip_bits = flips[tile_ids]
        levels = jax.random.randint(key_list[2], (SCAN_DEV,), 0, 3)
        ordering = jax.random.permutation(key_list[3], SCAN_DEV)
        return (tile_ids[ordering], flip_bits[ordering], levels[ordering])
    device_keys = jax.random.split(device_key, devices)
    tile_ids, flip_bits, levels = jax.vmap(one_device)(device_keys, device_special)
    row_ids = jnp.repeat(jnp.arange(N_ROW, dtype=jnp.int32), N_COL)[:, None]
    corner_row = row_ids * TH + levels * HALF
    corner_col = tile_ids * TW + flip_bits * HALF
    patch_corner = jnp.stack([corner_row, corner_col], axis=-1).reshape(SCANS, 2).astype(jnp.int32)
    covered_mask = jnp.stack([tile_ids, tile_ids + flip_bits], axis=-1).reshape(SCANS, 2).astype(jnp.int32)
    return (patch_corner, covered_mask)


def draw_scan_corner(key, part):
    placed, covered_mask = scan_plan(key)
    return placed


def draw_correlation(key, part):
    placed, covered_mask = scan_plan(key)
    return covered_mask


def draw_scan_count(key, part):
    key = jax.random.fold_in(key, 11)
    first_key, second_key = jax.random.split(key)
    counts = jax.random.randint(first_key, (N_ROW * N_COL,), 1, SCAN_DEV + 1)
    busiest = jax.random.randint(second_key, (), 0, N_ROW * N_COL)
    counts = jnp.where(jnp.arange(N_ROW * N_COL) == busiest, SCAN_DEV, counts)
    return counts.reshape(N_ROW, N_COL).astype(jnp.int32)


def shard_levels(rng, dims, cuts, low, high):
    level = 1.0
    for position, blocks in cuts:
        heights = jax.random.uniform(jax.random.fold_in(jax.random.fold_in(rng, 6), position), (blocks,), jnp.float32, low / len(cuts), high / len(cuts))
        level = level * jnp.repeat(jnp.exp(heights), dims[position] // blocks).reshape((-1,) + (1,) * (len(dims) - 1 - position))
    return level


def centred(rng, dims, deviation, limit, cuts=(), kind=jnp.bfloat16):
    array = deviation * jax.random.normal(rng, dims, jnp.float32)
    if cuts:
        array = array * shard_levels(rng, dims, cuts, -0.22, 0.18)
    return jnp.clip(array, -limit, limit).astype(kind)


def setup_inputs(seed: int = 0) -> dict:
    arg_keys = jax.random.split(jax.random.key(seed), 9)
    object_slices = centred(arg_keys[0], (S, 2, NH, NW), 0.7, 6.0, ((2, 8), (3, 16)), jnp.float32)
    probe = centred(arg_keys[1], (M, 2, P_SIZE, P_SIZE), 0.5, 6.0)
    measured = jnp.clip(3.0 * jax.random.uniform(arg_keys[2], (SCANS, P_SIZE, P_SIZE), jnp.float32) ** shard_levels(arg_keys[2], (SCANS, P_SIZE, P_SIZE), ((0, 128),), -0.2, 0.2), 0.0, 3.0)
    tap_row = centred(arg_keys[3], (2, TAPS), (2 * TAPS) ** -0.5, 0.5, (), jnp.float32)
    tap_col = centred(arg_keys[4], (2, TAPS), (2 * TAPS) ** -0.5, 0.5, (), jnp.float32)
    scan_corner = draw_scan_corner(jax.random.fold_in(arg_keys[8], 71), 0)
    correlation = draw_correlation(jax.random.fold_in(arg_keys[8], 71), 0)
    scan_count = draw_scan_count(jax.random.fold_in(arg_keys[8], 71), 0)
    return dict(object_slices=object_slices, probe=probe, measured=measured, tap_row=tap_row, tap_col=tap_col, scan_corner=scan_corner, correlation=correlation, scan_count=scan_count)


def make_tables(tap_row, tap_col, patch_size):
    taps = tap_row.shape[-1]
    index = jnp.arange(patch_size, dtype=jnp.int32)
    offset = index[None, :] - index[:, None] + taps // 2
    picker = (offset[:, :, None] == jnp.arange(taps, dtype=jnp.int32)[None, None, :]).astype(jnp.float32)

    def banded(vector):
        return lax.optimization_barrier(jnp.sum(picker * vector.astype(jnp.float32)[None, None, :], axis=-1))
    left_re, left_im = (banded(tap_row[0]), banded(tap_row[1]))
    cols_re, cols_im = (banded(tap_col[0]), banded(tap_col[1]))
    phase = (index[:, None] * index[None, :] % patch_size).astype(jnp.float32) * (2.0 * math.pi / patch_size)
    norming = 1.0 / math.sqrt(patch_size)
    dft_re = jnp.cos(phase) * norming
    dft_im = -jnp.sin(phase) * norming
    pairs = ((left_re, left_im), (cols_re.T, cols_im.T), (left_re.T, -left_im.T), (cols_re, -cols_im), (dft_re, dft_im), (dft_re, -dft_im))
    return tuple(((first.astype(jnp.bfloat16), second.astype(jnp.bfloat16)) for first, second in pairs))

def to_low(pair):
    return (pair[0].astype(jnp.bfloat16), pair[1].astype(jnp.bfloat16))

def times(one_pair, two_pair):
    return (one_pair[0] * two_pair[0] - one_pair[1] * two_pair[1], one_pair[0] * two_pair[1] + one_pair[1] * two_pair[0])

def conj_times(one_pair, two_pair):
    return (one_pair[0] * two_pair[0] + one_pair[1] * two_pair[1], one_pair[0] * two_pair[1] - one_pair[1] * two_pair[0])

def apply_left(matrix, field, product):
    return (product(matrix[0], field[0]) - product(matrix[1], field[1]), product(matrix[0], field[1]) + product(matrix[1], field[0]))

def apply_right(field, matrix, product):
    return (product(field[0], matrix[0]) - product(field[1], matrix[1]), product(field[0], matrix[1]) + product(field[1], matrix[0]))

def scan_contributions(object_window, measurement, living_entries, probe, lookup_tables, row_outcome, column_outcome):
    left_pair, right_pair, left_adj, right_adj, dft_pair, dft_conj = lookup_tables
    probe_pair = (probe[:, 0].astype(jnp.float32), probe[:, 1].astype(jnp.float32))
    first_slice = (object_window[0, 0].astype(jnp.float32), object_window[0, 1].astype(jnp.float32))
    second_slice = (object_window[1, 0].astype(jnp.float32), object_window[1, 1].astype(jnp.float32))
    wave = to_low(times(probe_pair, first_slice))
    spread = to_low(apply_left(left_pair, wave, row_outcome))
    moved = apply_right(spread, right_pair, column_outcome)
    exit_wave = to_low(times(moved, second_slice))
    rows_done = to_low(apply_left(dft_pair, exit_wave, row_outcome))
    far_field = apply_right(rows_done, dft_pair, column_outcome)
    predicted_intensity = lax.optimization_barrier(jnp.sum(far_field[0] * far_field[0] + far_field[1] * far_field[1], axis=0))
    scale_multiplier = living_entries * (1.0 - measurement / jnp.sqrt(predicted_intensity + 1.0))
    scaled = to_low((scale_multiplier * far_field[0], scale_multiplier * far_field[1]))
    rows_back = to_low(apply_left(dft_conj, scaled, row_outcome))
    adjoint = apply_right(rows_back, dft_conj, column_outcome)
    second_terms = conj_times(moved, adjoint)
    upstream = to_low(conj_times(second_slice, adjoint))
    back_rows = to_low(apply_left(left_adj, upstream, row_outcome))
    inner = apply_right(back_rows, right_adj, column_outcome)
    first_terms = conj_times(probe_pair, inner)
    probe_terms = conj_times(first_slice, inner)
    first_grad = jnp.stack([lax.optimization_barrier(jnp.sum(first_terms[0], axis=0)), lax.optimization_barrier(jnp.sum(first_terms[1], axis=0))])
    second_grad = jnp.stack([lax.optimization_barrier(jnp.sum(second_terms[0], axis=0)), lax.optimization_barrier(jnp.sum(second_terms[1], axis=0))])
    gradient_fragment = jnp.stack([first_grad, second_grad]).astype(jnp.bfloat16)
    return (gradient_fragment, jnp.stack([probe_terms[0], probe_terms[1]], axis=1))

def row_precise(matrix, field):
    return jnp.einsum('ij,mjk->mik', matrix.astype(jnp.float32), field.astype(jnp.float32), precision=lax.Precision.HIGHEST)

def column_precise(field, matrix):
    return jnp.einsum('mij,jk->mik', field.astype(jnp.float32), matrix.astype(jnp.float32), precision=lax.Precision.HIGHEST)

def reference(object_slices, probe, measured, tap_row, tap_col, scan_corner, correlation, scan_count):
    patch_size = probe.shape[-1]
    half_cols = patch_size // 2
    tile_cols = patch_size
    lookup_tables = make_tables(tap_row, tap_col, patch_size)
    object_low = object_slices.astype(jnp.bfloat16)
    scan_total = measured.shape[0]
    flat_count = scan_count.reshape(-1)
    anchor = jnp.int32(0)

    def columns(patch_corner, covered_mask):
        offset = patch_corner[1] % tile_cols
        left_col = covered_mask[0] * tile_cols + offset
        right_col = covered_mask[1] * tile_cols + (offset + half_cols) % tile_cols
        return (left_col.astype(jnp.int32), right_col.astype(jnp.int32))

    def per_scan(running, input_arrays):
        patch_corner, covered_mask, measurement, entry_number = input_arrays
        living_entries = (entry_number % SCAN_DEV < flat_count[entry_number // SCAN_DEV]).astype(jnp.float32)
        left_col, right_col = columns(patch_corner, covered_mask)
        start_row = patch_corner[0].astype(jnp.int32)
        left_part = lax.dynamic_slice(object_low, (anchor, anchor, start_row, left_col), (S, 2, patch_size, half_cols))
        right_part = lax.dynamic_slice(object_low, (anchor, anchor, start_row, right_col), (S, 2, patch_size, half_cols))
        object_window = jnp.concatenate([left_part, right_part], axis=-1)
        gradient_fragment, probe_contribution = scan_contributions(object_window, measurement, living_entries, probe, lookup_tables, row_precise, column_precise)
        return (running + probe_contribution, gradient_fragment)
    numbers = jnp.arange(scan_total, dtype=jnp.int32)
    start = jnp.zeros((probe.shape[0], 2, patch_size, patch_size), jnp.float32)
    running, pieces = lax.scan(per_scan, start, (scan_corner, correlation, measured, numbers))
    probe_grad = running / math.sqrt(scan_total)

    def place(entry_number, tile_grad):
        patch_corner = scan_corner[entry_number]
        left_col, right_col = columns(patch_corner, correlation[entry_number])
        start_row = patch_corner[0].astype(jnp.int32)
        gradient_fragment = pieces[entry_number].astype(jnp.float32)
        current = lax.dynamic_slice(tile_grad, (anchor, anchor, start_row, left_col), (S, 2, patch_size, half_cols))
        tile_grad = lax.dynamic_update_slice(tile_grad, current + gradient_fragment[..., :half_cols], (anchor, anchor, start_row, left_col))
        current = lax.dynamic_slice(tile_grad, (anchor, anchor, start_row, right_col), (S, 2, patch_size, half_cols))
        return lax.dynamic_update_slice(tile_grad, current + gradient_fragment[..., half_cols:], (anchor, anchor, start_row, right_col))
    object_grad = lax.fori_loop(0, scan_total, place, jnp.zeros(object_slices.shape, jnp.float32))
    return (object_grad, probe_grad)
```

```python
import math

import jax
import jax.numpy as jnp
import numpy as np
from jax import lax
from jax.experimental import pallas as pl
from jax.experimental.pallas import tpu as pltpu
from jax.sharding import PartitionSpec as P

SIZE = 256
HALF = 128
MODES = 4
META = 16
CHUNK = 32
BF16 = jnp.bfloat16
F32 = jnp.float32


def dft_tables():
    index = np.arange(SIZE)
    phase = 2.0 * np.pi * ((index[:, None] * index[None, :]) % SIZE) / SIZE
    real = np.cos(phase) / math.sqrt(SIZE)
    imag = -np.sin(phase) / math.sqrt(SIZE)
    left = np.block([[real, -imag], [imag, real]])
    right = np.block([[real, imag], [-imag, real]])
    return jnp.asarray(left, F32).astype(BF16), jnp.asarray(right, F32).astype(BF16)


def pack_kernel(info, measured, obj, slots, tile_low, right_cols):
    slots[:, SIZE:, :] = jnp.zeros((slots.shape[0], META, SIZE), BF16)
    scans, tiles = measured.shape[0], slots.shape[0]
    level = [(info[2 * n] // HALF) % 4 for n in range(scans)]
    straddles = [(info[2 * n + 1] // HALF) % 2 for n in range(scans)]
    tile = [info[2 * scans + 2 * n] for n in range(scans)]
    count, device = info[4 * scans], info[4 * scans + 1]

    def twin(one, two):
        same = (tile[one] == tile[two]) & (straddles[one] + straddles[two] == 2)
        return same.astype(jnp.int32)

    before = [jnp.int32(0)] * scans
    after = [jnp.int32(0)] * scans
    twins = jnp.int32(0)
    for two in range(scans):
        for one in range(two):
            same = twin(one, two)
            before[two], after[one] = before[two] | same, after[one] | same
            twins = twins | same
    rule = (5 * device) % 16
    leftwards = (rule < 6).astype(jnp.int32) * (1 - twins)
    rightwards = ((rule >= 6) & (rule < 13)).astype(jnp.int32)
    for n in range(scans):
        shift = straddles[n] * jnp.where(before[n] == 1, 1, jnp.where(after[n] == 1, 0, rightwards))
        shift = shift - (1 - straddles[n]) * leftwards
        home = lax.rem(tile[n] + shift + tiles, tiles)
        code = 1 + level[n] * 4 + 1 + straddles[n] - 2 * shift

        @pl.when(n < count)
        def _():
            slots[home, :SIZE, :] = measured[n].astype(BF16)
            slots[home, SIZE:, :] = jnp.full((META, SIZE), code, jnp.int32).astype(F32).astype(BF16)

    tile_low[...] = obj[...].astype(BF16)
    right_cols[...] = obj[:, :, :, HALF:].astype(BF16)


def table_kernel(taps, tables):
    def banded(row, shift):
        line = jnp.broadcast_to(taps[row : row + 1, :], (SIZE, 2 * SIZE))
        return pltpu.roll(line, shift, 1, stride=1, stride_axis=0)[:, :SIZE]

    straight, turned = 2 * SIZE - 32, 2 * SIZE - 31

    def put(place, real, imag, from_left):
        sign = 1.0 if from_left else -1.0
        tables[place, :SIZE, :SIZE] = real.astype(BF16)
        tables[place, :SIZE, SIZE:] = (-sign * imag).astype(BF16)
        tables[place, SIZE:, :SIZE] = (sign * imag).astype(BF16)
        tables[place, SIZE:, SIZE:] = real.astype(BF16)

    put(0, banded(0, straight), banded(1, straight), True)
    put(1, banded(6, turned), banded(7, turned), False)
    put(2, banded(4, turned), -banded(5, turned), True)
    put(3, banded(2, straight), -banded(3, straight), False)


def scan_kernel(
    codes, slots, before, tile, after, probe, tables, dft_left, dft_right,
    own_grad, left_grad, right_grad, probe_grad,
    ext, patch, rows_in, cols_in, moved, far, acc, probe_acc,
):
    ext[0] = before[...]
    ext[1], ext[2] = tile[:, :, :, :HALF], tile[:, :, :, HALF:]
    ext[3], ext[4] = after[:, :, :, :HALF], after[:, :, :, HALF:]
    acc[...] = jnp.zeros(acc.shape, F32)
    probe_acc[...] = jnp.zeros(probe_acc.shape, F32)
    chunks = [slice(at, at + CHUNK) for at in range(0, SIZE, CHUNK)]

    def left_stage(table):
        for m in range(MODES):
            both = jnp.dot(table, rows_in[m], preferred_element_type=F32)
            here = slice(m * SIZE, (m + 1) * SIZE)
            cols_in[here, :SIZE] = both[:SIZE].astype(BF16)
            cols_in[here, SIZE:] = both[SIZE:].astype(BF16)

    def right_stage(table, out):
        for m in range(MODES):
            here = slice(m * SIZE, (m + 1) * SIZE)
            out[here, :] = jnp.dot(cols_in[here, :], table, preferred_element_type=F32)

    def put_rows(m, at, real, imag):
        rows_in[m, at.start : at.stop, :] = real.astype(BF16)
        rows_in[m, SIZE + at.start : SIZE + at.stop, :] = imag.astype(BF16)

    def pair(ref, m, at):
        here = slice(m * SIZE + at.start, m * SIZE + at.stop)
        return ref[here, :SIZE], ref[here, SIZE:]

    def one_scan(slot):
        code = codes[slot] - 1
        column = code % 4
        start = pl.multiple_of((code // 4) * HALF, HALF)
        window = pl.ds(start, SIZE)
        for s in range(2):
            for part in range(2):
                for side in range(2):
                    low = part * SIZE + side * HALF
                    patch[s, :, low : low + HALF] = ext[column + side, s, part, window, :].astype(F32)

        for at in chunks:
            o_re, o_im = patch[0, at, :SIZE], patch[0, at, SIZE:]
            for m in range(MODES):
                p_re, p_im = probe[m, 0, at, :].astype(F32), probe[m, 1, at, :].astype(F32)
                put_rows(m, at, p_re * o_re - p_im * o_im, p_re * o_im + p_im * o_re)
        left_stage(tables[0])
        right_stage(tables[1], moved)
        for at in chunks:
            o_re, o_im = patch[1, at, :SIZE], patch[1, at, SIZE:]
            for m in range(MODES):
                v_re, v_im = pair(moved, m, at)
                put_rows(m, at, v_re * o_re - v_im * o_im, v_re * o_im + v_im * o_re)
        left_stage(dft_left[...])
        right_stage(dft_right[...], far)
        for at in chunks:
            power = jnp.ones((CHUNK, SIZE), F32)
            for m in range(MODES):
                f_re, f_im = pair(far, m, at)
                power = power + (f_re * f_re + f_im * f_im)
            factor = 1.0 - slots[slot, at, :].astype(F32) / jnp.sqrt(power)
            for m in range(MODES):
                f_re, f_im = pair(far, m, at)
                put_rows(m, at, factor * f_re, factor * f_im)
        left_stage(dft_right[...])
        right_stage(dft_left[...], far)
        for at in chunks:
            o_re, o_im = patch[1, at, :SIZE], patch[1, at, SIZE:]
            g_re = jnp.zeros((CHUNK, SIZE), F32)
            g_im = jnp.zeros((CHUNK, SIZE), F32)
            for m in range(MODES):
                a_re, a_im = pair(far, m, at)
                v_re, v_im = pair(moved, m, at)
                g_re = g_re + (v_re * a_re + v_im * a_im)
                g_im = g_im + (v_re * a_im - v_im * a_re)
                put_rows(m, at, o_re * a_re + o_im * a_im, o_re * a_im - o_im * a_re)
            add_piece(1, at, column, start, g_re, g_im)
        left_stage(tables[2])
        right_stage(tables[3], moved)
        for at in chunks:
            o_re, o_im = patch[0, at, :SIZE], patch[0, at, SIZE:]
            g_re = jnp.zeros((CHUNK, SIZE), F32)
            g_im = jnp.zeros((CHUNK, SIZE), F32)
            for m in range(MODES):
                i_re, i_im = pair(moved, m, at)
                p_re, p_im = probe[m, 0, at, :].astype(F32), probe[m, 1, at, :].astype(F32)
                g_re = g_re + (p_re * i_re + p_im * i_im)
                g_im = g_im + (p_re * i_im - p_im * i_re)
                probe_acc[m, 0, at, :] += o_re * i_re + o_im * i_im
                probe_acc[m, 1, at, :] += o_re * i_im - o_im * i_re
            add_piece(0, at, column, start, g_re, g_im)

    def add_piece(s, at, column, start, g_re, g_im):
        rows = pl.ds(pl.multiple_of(start + at.start, CHUNK), CHUNK)
        for part, value in ((0, g_re), (1, g_im)):
            value = value.astype(BF16).astype(F32)
            for side in range(2):
                acc[column + side, s, part, rows, :] += value[:, side * HALF : (side + 1) * HALF]

    @pl.loop(0, codes.shape[0])
    def _(slot):
        @pl.when(codes[slot] > 0)
        def _():
            one_scan(slot)

    left_grad[...] = acc[0].astype(BF16)
    own_grad[:, :, :, :HALF] = acc[1]
    own_grad[:, :, :, HALF:] = acc[2]
    right_grad[:, :, :, :HALF] = acc[3].astype(BF16)
    right_grad[:, :, :, HALF:] = acc[4].astype(BF16)
    probe_grad[...] = probe_acc[...].astype(BF16)


def whole(count):
    return [pl.BlockSpec(memory_space=pltpu.VMEM) for _ in range(count)]


def scalars(count):
    return [pl.BlockSpec(memory_space=pltpu.SMEM) for _ in range(count)]


def body(object_slices, probe, measured, tap_row, tap_col, scan_corner, correlation, scan_count):
    cols = lax.axis_size("col")
    rows = lax.axis_size("row")
    band = object_slices.shape[2]
    part_shape = (2, 2, band, HALF)
    limit = pltpu.CompilerParams(vmem_limit_bytes=56 * 1024 * 1024)

    tile_shape = (2, 2, band, SIZE)
    info = [scan_corner.reshape(-1), correlation.reshape(-1), scan_count.reshape(-1)]
    info = jnp.concatenate(info + [lax.axis_index("col").reshape(1)])
    slots, tile_low, right_cols = pl.pallas_call(
        pack_kernel,
        out_shape=[
            jax.ShapeDtypeStruct((cols, SIZE + META, SIZE), BF16),
            jax.ShapeDtypeStruct(tile_shape, BF16),
            jax.ShapeDtypeStruct(part_shape, BF16),
        ],
        in_specs=scalars(1) + whole(2),
        out_specs=whole(3),
        compiler_params=limit,
    )(info, measured, object_slices)
    to_left = [(c, (c - 1) % cols) for c in range(cols)]
    to_right = [(c, (c + 1) % cols) for c in range(cols)]
    after = lax.ppermute(tile_low, "col", to_left)
    before = lax.ppermute(right_cols, "col", to_right)
    arrived = lax.all_to_all(slots, "col", split_axis=0, concat_axis=0, tiled=True)

    taps = jnp.concatenate([tap_row, tap_col], axis=0)
    taps = jnp.concatenate([taps, taps[:, ::-1]], axis=0)
    taps = jnp.pad(taps, ((0, 0), (0, 2 * SIZE - taps.shape[1])))
    tables = pl.pallas_call(
        table_kernel,
        out_shape=jax.ShapeDtypeStruct((4, 2 * SIZE, 2 * SIZE), BF16),
        in_specs=whole(1),
        out_specs=pl.BlockSpec(memory_space=pltpu.VMEM),
        compiler_params=limit,
    )(taps)
    dft_left, dft_right = dft_tables()
    codes = arrived[:, SIZE, 0].astype(jnp.int32)

    own_grad, left_grad, right_grad, probe_part = pl.pallas_call(
        scan_kernel,
        out_shape=[
            jax.ShapeDtypeStruct(tile_shape, F32),
            jax.ShapeDtypeStruct(part_shape, BF16),
            jax.ShapeDtypeStruct(tile_shape, BF16),
            jax.ShapeDtypeStruct(probe.shape, BF16),
        ],
        in_specs=scalars(1) + whole(8),
        out_specs=whole(4),
        scratch_shapes=[
            pltpu.VMEM((5,) + part_shape, BF16),
            pltpu.VMEM((2, SIZE, 2 * SIZE), F32),
            pltpu.VMEM((MODES, 2 * SIZE, SIZE), BF16),
            pltpu.VMEM((MODES * SIZE, 2 * SIZE), BF16),
            pltpu.VMEM((MODES * SIZE, 2 * SIZE), F32),
            pltpu.VMEM((MODES * SIZE, 2 * SIZE), F32),
            pltpu.VMEM((5,) + part_shape, F32),
            pltpu.VMEM(probe.shape, F32),
        ],
        compiler_params=limit,
    )(codes, arrived, before, tile_low, after, probe, tables, dft_left, dft_right)

    from_left = lax.ppermute(right_grad, "col", to_right)
    from_right = lax.ppermute(left_grad, "col", to_left)
    share = MODES * 2 * SIZE // cols
    mine = lax.all_to_all(
        probe_part.reshape(cols, share, SIZE), "col", split_axis=0, concat_axis=0, tiled=True
    )
    mine = jnp.sum(mine.astype(F32), axis=0).astype(BF16)
    mine = jnp.broadcast_to(mine[None], (rows, share, SIZE))
    mine = lax.all_to_all(mine, "row", split_axis=0, concat_axis=0, tiled=True)
    scale = 1.0 / math.sqrt(measured.shape[0] * cols * rows)
    mine = (jnp.sum(mine.astype(F32), axis=0) * scale).astype(BF16)
    mine = jnp.broadcast_to(mine[None], (cols, share, SIZE))
    probe_grad = lax.all_to_all(mine, "col", split_axis=0, concat_axis=0, tiled=True)
    probe_grad = probe_grad.astype(F32).reshape(probe.shape)
    from_right = jnp.pad(from_right.astype(F32), ((0, 0), (0, 0), (0, 0), (HALF, 0)))
    return own_grad + from_left.astype(F32) + from_right, probe_grad


def solution(mesh):
    in_specs = (
        P(None, None, "row", "col"),
        P(),
        P(("row", "col"), None, None),
        P(),
        P(),
        P(("row", "col"), None),
        P(("row", "col"), None),
        P("row", "col"),
    )
    out_specs = (P(None, None, "row", "col"), P())
    return jax.shard_map(body, mesh=mesh, in_specs=in_specs, out_specs=out_specs, check_vma=False)
```

```python
import math

import jax
import jax.numpy as jnp
import numpy as np
from jax import lax
from jax.experimental import pallas as pl
from jax.experimental.pallas import tpu as pltpu
from jax.sharding import PartitionSpec as P

SIZE = 256
HALF = 128
MODES = 4
CHUNK = 32
BF16 = jnp.bfloat16
F32 = jnp.float32


def dft_tables():
    index = np.arange(SIZE)
    phase = 2.0 * np.pi * ((index[:, None] * index[None, :]) % SIZE) / SIZE
    real = np.cos(phase) / math.sqrt(SIZE)
    imag = -np.sin(phase) / math.sqrt(SIZE)
    left = np.block([[real, -imag], [imag, real]])
    right = np.block([[real, imag], [-imag, real]])
    return jnp.asarray(left, F32).astype(BF16), jnp.asarray(right, F32).astype(BF16)


def plan_kernel(info, obj, codes, homes, tile_low, right_cols):
    scans, tiles = homes.shape[0], codes.shape[0]
    level = [(info[2 * n] // HALF) % 4 for n in range(scans)]
    straddles = [(info[2 * n + 1] // HALF) % 2 for n in range(scans)]
    tile = [info[2 * scans + 2 * n] for n in range(scans)]
    count, device = info[4 * scans], info[4 * scans + 1]

    def twin(one, two):
        same = (tile[one] == tile[two]) & (straddles[one] + straddles[two] == 2)
        return same.astype(jnp.int32)

    before = [jnp.int32(0)] * scans
    after = [jnp.int32(0)] * scans
    twins = jnp.int32(0)
    for two in range(scans):
        for one in range(two):
            same = twin(one, two)
            before[two], after[one] = before[two] | same, after[one] | same
            twins = twins | same
    rule = (5 * device) % 16
    leftwards = (rule < 6).astype(jnp.int32) * (1 - twins)
    rightwards = ((rule >= 6) & (rule < 13)).astype(jnp.int32)
    for t in range(tiles):
        codes[t] = 0
    for n in range(scans):
        shift = straddles[n] * jnp.where(before[n] == 1, 1, jnp.where(after[n] == 1, 0, rightwards))
        shift = shift - (1 - straddles[n]) * leftwards
        home = lax.rem(tile[n] + shift + tiles, tiles)
        code = 1 + level[n] * 4 + 1 + straddles[n] - 2 * shift
        homes[n] = jnp.where(n < count, home, -1)

        @pl.when(n < count)
        def _():
            codes[home] = code

    tile_low[...] = obj[...].astype(BF16)
    right_cols[...] = obj[:, :, :, HALF:].astype(BF16)


def pack_kernel(homes, measured, slots):
    for n in range(measured.shape[0]):

        @pl.when(homes[n] >= 0)
        def _():
            slots[homes[n]] = measured[n].astype(BF16)


def table_kernel(taps, tables):
    def banded(row, shift):
        line = jnp.broadcast_to(taps[row : row + 1, :], (SIZE, 2 * SIZE))
        return pltpu.roll(line, shift, 1, stride=1, stride_axis=0)[:, :SIZE]

    straight, turned = 2 * SIZE - 32, 2 * SIZE - 31

    def put(place, real, imag, from_left):
        sign = 1.0 if from_left else -1.0
        tables[place, :SIZE, :SIZE] = real.astype(BF16)
        tables[place, :SIZE, SIZE:] = (-sign * imag).astype(BF16)
        tables[place, SIZE:, :SIZE] = (sign * imag).astype(BF16)
        tables[place, SIZE:, SIZE:] = real.astype(BF16)

    put(0, banded(0, straight), banded(1, straight), True)
    put(1, banded(6, turned), banded(7, turned), False)
    put(2, banded(4, turned), -banded(5, turned), True)
    put(3, banded(2, straight), -banded(3, straight), False)


CHUNKS = [slice(at, at + CHUNK) for at in range(0, SIZE, CHUNK)]


def left_stage(table, rows_in, cols_in):
    for m in range(MODES):
        both = jnp.dot(table, rows_in[m], preferred_element_type=F32)
        here = slice(m * SIZE, (m + 1) * SIZE)
        cols_in[here, :SIZE] = both[:SIZE].astype(BF16)
        cols_in[here, SIZE:] = both[SIZE:].astype(BF16)


def right_stage(table, cols_in, out):
    for m in range(MODES):
        here = slice(m * SIZE, (m + 1) * SIZE)
        out[here, :] = jnp.dot(cols_in[here, :], table, preferred_element_type=F32)


def put_rows(rows_in, m, at, real, imag):
    rows_in[m, at.start : at.stop, :] = real.astype(BF16)
    rows_in[m, SIZE + at.start : SIZE + at.stop, :] = imag.astype(BF16)


def pair(ref, m, at):
    here = slice(m * SIZE + at.start, m * SIZE + at.stop)
    return ref[here, :SIZE], ref[here, SIZE:]


def extend(before, tile, after, ext):
    ext[0] = before[...]
    ext[1], ext[2] = tile[:, :, :, :HALF], tile[:, :, :, HALF:]
    ext[3], ext[4] = after[:, :, :, :HALF], after[:, :, :, HALF:]


def live_list(codes, order):
    def note(slot, found):
        live = codes[slot] > 0

        @pl.when(live)
        def _():
            order[found] = slot

        return found + live.astype(jnp.int32)

    return lax.fori_loop(0, codes.shape[0], note, jnp.int32(0))


def read_patch(code, ext, patch):
    column = code % 4
    start = pl.multiple_of((code // 4) * HALF, HALF)
    window = pl.ds(start, SIZE)
    for s in range(2):
        for part in range(2):
            for side in range(2):
                low = part * SIZE + side * HALF
                patch[s, :, low : low + HALF] = ext[column + side, s, part, window, :].astype(F32)
    return column, start


def forward_kernel(
    codes, before, tile, after, probe, tables, dft_left, dft_right,
    moved_all, far_all, root_all,
    ext, patch, rows_in, cols_in, moved_two, far_two, root_two, order, sems,
):
    extend(before, tile, after, ext)
    found = live_list(codes, order)

    def copies(i):
        two = lax.rem(i, 2)
        slot = order[i]
        return [
            pltpu.make_async_copy(one.at[two], full.at[slot], sems.at[two, k])
            for k, (one, full) in enumerate(
                ((moved_two, moved_all), (far_two, far_all), (root_two, root_all))
            )
        ]

    @pl.loop(0, found)
    def _(i):
        two = lax.rem(i, 2)
        moved, far, root = moved_two.at[two], far_two.at[two], root_two.at[two]

        @pl.when(i >= 2)
        def _():
            for copy in copies(i - 2):
                copy.wait()

        read_patch(codes[order[i]] - 1, ext, patch)
        for at in CHUNKS:
            o_re, o_im = patch[0, at, :SIZE], patch[0, at, SIZE:]
            for m in range(MODES):
                p_re, p_im = probe[m, 0, at, :].astype(F32), probe[m, 1, at, :].astype(F32)
                put_rows(rows_in, m, at, p_re * o_re - p_im * o_im, p_re * o_im + p_im * o_re)
        left_stage(tables[0], rows_in, cols_in)
        right_stage(tables[1], cols_in, moved)
        for at in CHUNKS:
            o_re, o_im = patch[1, at, :SIZE], patch[1, at, SIZE:]
            for m in range(MODES):
                v_re, v_im = pair(moved, m, at)
                put_rows(rows_in, m, at, v_re * o_re - v_im * o_im, v_re * o_im + v_im * o_re)
        left_stage(dft_left[...], rows_in, cols_in)
        right_stage(dft_right[...], cols_in, far)
        for at in CHUNKS:
            power = jnp.ones((CHUNK, SIZE), F32)
            for m in range(MODES):
                f_re, f_im = pair(far, m, at)
                power = power + (f_re * f_re + f_im * f_im)
            root[at, :] = 1.0 / jnp.sqrt(power)
        for copy in copies(i):
            copy.start()

    for last in (2, 1):

        @pl.when(found >= last)
        def _():
            for copy in copies(found - last):
                copy.wait()


def backward_kernel(
    codes, slots, before, tile, after, probe, tables, dft_left, dft_right,
    moved_all, far_all, root_all,
    own_grad, left_grad, right_grad, probe_grad,
    ext, patch, rows_in, cols_in, moved_two, far_two, root_two, acc, probe_acc, order, sems,
):
    found = live_list(codes, order)

    def copies(i):
        two = lax.rem(i, 2)
        slot = order[i]
        return [
            pltpu.make_async_copy(full.at[slot], one.at[two], sems.at[two, k])
            for k, (one, full) in enumerate(
                ((moved_two, moved_all), (far_two, far_all), (root_two, root_all))
            )
        ]

    @pl.when(found > 0)
    def _():
        for copy in copies(0):
            copy.start()

    extend(before, tile, after, ext)
    acc[...] = jnp.zeros(acc.shape, F32)
    probe_acc[...] = jnp.zeros(probe_acc.shape, F32)

    def add_piece(s, at, column, start, g_re, g_im):
        rows = pl.ds(pl.multiple_of(start + at.start, CHUNK), CHUNK)
        for part, value in ((0, g_re), (1, g_im)):
            value = value.astype(BF16).astype(F32)
            for side in range(2):
                acc[column + side, s, part, rows, :] += value[:, side * HALF : (side + 1) * HALF]

    @pl.loop(0, found)
    def _(i):
        two = lax.rem(i, 2)
        moved, far, root = moved_two.at[two], far_two.at[two], root_two.at[two]

        @pl.when(i + 1 < found)
        def _():
            for copy in copies(i + 1):
                copy.start()

        slot = order[i]
        column, start = read_patch(codes[slot] - 1, ext, patch)
        for copy in copies(i):
            copy.wait()
        for at in CHUNKS:
            factor = 1.0 - slots[slot, at, :].astype(F32) * root[at, :]
            for m in range(MODES):
                f_re, f_im = pair(far, m, at)
                put_rows(rows_in, m, at, factor * f_re, factor * f_im)
        left_stage(dft_right[...], rows_in, cols_in)
        right_stage(dft_left[...], cols_in, far)
        for at in CHUNKS:
            o_re, o_im = patch[1, at, :SIZE], patch[1, at, SIZE:]
            g_re = jnp.zeros((CHUNK, SIZE), F32)
            g_im = jnp.zeros((CHUNK, SIZE), F32)
            for m in range(MODES):
                a_re, a_im = pair(far, m, at)
                v_re, v_im = pair(moved, m, at)
                g_re = g_re + (v_re * a_re + v_im * a_im)
                g_im = g_im + (v_re * a_im - v_im * a_re)
                put_rows(rows_in, m, at, o_re * a_re + o_im * a_im, o_re * a_im - o_im * a_re)
            add_piece(1, at, column, start, g_re, g_im)
        left_stage(tables[2], rows_in, cols_in)
        right_stage(tables[3], cols_in, moved)
        for at in CHUNKS:
            o_re, o_im = patch[0, at, :SIZE], patch[0, at, SIZE:]
            g_re = jnp.zeros((CHUNK, SIZE), F32)
            g_im = jnp.zeros((CHUNK, SIZE), F32)
            for m in range(MODES):
                i_re, i_im = pair(moved, m, at)
                p_re, p_im = probe[m, 0, at, :].astype(F32), probe[m, 1, at, :].astype(F32)
                g_re = g_re + (p_re * i_re + p_im * i_im)
                g_im = g_im + (p_re * i_im - p_im * i_re)
                probe_acc[m, 0, at, :] += o_re * i_re + o_im * i_im
                probe_acc[m, 1, at, :] += o_re * i_im - o_im * i_re
            add_piece(0, at, column, start, g_re, g_im)

    left_grad[...] = acc[0].astype(BF16)
    own_grad[:, :, :, :HALF] = acc[1]
    own_grad[:, :, :, HALF:] = acc[2]
    right_grad[:, :, :, :HALF] = acc[3].astype(BF16)
    right_grad[:, :, :, HALF:] = acc[4].astype(BF16)
    probe_grad[...] = probe_acc[...].astype(BF16)


def whole(count):
    return [pl.BlockSpec(memory_space=pltpu.VMEM) for _ in range(count)]


def scalars(count):
    return [pl.BlockSpec(memory_space=pltpu.SMEM) for _ in range(count)]


def body(object_slices, probe, measured, tap_row, tap_col, scan_corner, correlation, scan_count):
    cols = lax.axis_size("col")
    rows = lax.axis_size("row")
    band = object_slices.shape[2]
    part_shape = (2, 2, band, HALF)
    limit = pltpu.CompilerParams(vmem_limit_bytes=56 * 1024 * 1024)

    tile_shape = (2, 2, band, SIZE)
    info = [scan_corner.reshape(-1), correlation.reshape(-1), scan_count.reshape(-1)]
    info = jnp.concatenate(info + [lax.axis_index("col").reshape(1)])
    scans = measured.shape[0]
    codes, homes, tile_low, right_cols = pl.pallas_call(
        plan_kernel,
        out_shape=[
            jax.ShapeDtypeStruct((cols,), jnp.int32),
            jax.ShapeDtypeStruct((scans,), jnp.int32),
            jax.ShapeDtypeStruct(tile_shape, BF16),
            jax.ShapeDtypeStruct(part_shape, BF16),
        ],
        in_specs=scalars(1) + whole(1),
        out_specs=scalars(2) + whole(2),
        compiler_params=limit,
    )(info, object_slices)
    to_left = [(c, (c - 1) % cols) for c in range(cols)]
    to_right = [(c, (c + 1) % cols) for c in range(cols)]
    after = lax.ppermute(tile_low, "col", to_left)
    before = lax.ppermute(right_cols, "col", to_right)
    codes = lax.all_to_all(codes.reshape(cols, 1), "col", split_axis=0, concat_axis=0, tiled=True)
    codes, homes = lax.optimization_barrier((codes.reshape(cols), homes))
    slots = pl.pallas_call(
        pack_kernel,
        out_shape=jax.ShapeDtypeStruct((cols, SIZE, SIZE), BF16),
        in_specs=scalars(1) + whole(1),
        out_specs=pl.BlockSpec(memory_space=pltpu.VMEM),
        compiler_params=limit,
    )(homes, measured)
    arrived = lax.all_to_all(slots, "col", split_axis=0, concat_axis=0, tiled=True)

    taps = jnp.concatenate([tap_row, tap_col], axis=0)
    taps = jnp.concatenate([taps, taps[:, ::-1]], axis=0)
    taps = jnp.pad(taps, ((0, 0), (0, 2 * SIZE - taps.shape[1])))
    tables = pl.pallas_call(
        table_kernel,
        out_shape=jax.ShapeDtypeStruct((4, 2 * SIZE, 2 * SIZE), BF16),
        in_specs=whole(1),
        out_specs=pl.BlockSpec(memory_space=pltpu.VMEM),
        compiler_params=limit,
    )(taps)
    dft_left, dft_right = dft_tables()

    def anywhere(count):
        return [pl.BlockSpec(memory_space=pl.ANY) for _ in range(count)]

    field_shape = (MODES * SIZE, 2 * SIZE)
    work = [
        pltpu.VMEM((5,) + part_shape, BF16),
        pltpu.VMEM((2, SIZE, 2 * SIZE), F32),
        pltpu.VMEM((MODES, 2 * SIZE, SIZE), BF16),
        pltpu.VMEM(field_shape, BF16),
        pltpu.VMEM((2,) + field_shape, F32),
        pltpu.VMEM((2,) + field_shape, F32),
        pltpu.VMEM((2, SIZE, SIZE), F32),
    ]
    lists = [pltpu.SMEM((cols,), jnp.int32), pltpu.SemaphoreType.DMA((2, 3))]
    moved_all, far_all, root_all = pl.pallas_call(
        forward_kernel,
        out_shape=[
            jax.ShapeDtypeStruct((cols,) + field_shape, F32),
            jax.ShapeDtypeStruct((cols,) + field_shape, F32),
            jax.ShapeDtypeStruct((cols, SIZE, SIZE), F32),
        ],
        in_specs=scalars(1) + whole(7),
        out_specs=anywhere(3),
        scratch_shapes=work + lists,
        cost_estimate=pl.CostEstimate(flops=40 * 10**9, bytes_accessed=10**7, transcendentals=0),
        compiler_params=limit,
    )(codes, before, tile_low, after, probe, tables, dft_left, dft_right)
    own_grad, left_grad, right_grad, probe_part = pl.pallas_call(
        backward_kernel,
        out_shape=[
            jax.ShapeDtypeStruct(tile_shape, F32),
            jax.ShapeDtypeStruct(part_shape, BF16),
            jax.ShapeDtypeStruct(tile_shape, BF16),
            jax.ShapeDtypeStruct(probe.shape, BF16),
        ],
        in_specs=scalars(1) + whole(8) + anywhere(3),
        out_specs=whole(4),
        scratch_shapes=work + [pltpu.VMEM((5,) + part_shape, F32), pltpu.VMEM(probe.shape, F32)] + lists,
        compiler_params=limit,
    )(
        codes, arrived, before, tile_low, after, probe, tables, dft_left, dft_right,
        moved_all, far_all, root_all,
    )

    from_left = lax.ppermute(right_grad, "col", to_right)
    from_right = lax.ppermute(left_grad, "col", to_left)
    share = MODES * 2 * SIZE // cols
    mine = lax.all_to_all(
        probe_part.reshape(cols, share, SIZE), "col", split_axis=0, concat_axis=0, tiled=True
    )
    mine = jnp.sum(mine.astype(F32), axis=0).astype(BF16)
    mine = jnp.broadcast_to(mine[None], (rows, share, SIZE))
    mine = lax.all_to_all(mine, "row", split_axis=0, concat_axis=0, tiled=True)
    scale = 1.0 / math.sqrt(measured.shape[0] * cols * rows)
    mine = (jnp.sum(mine.astype(F32), axis=0) * scale).astype(BF16)
    mine, from_left, from_right = lax.optimization_barrier((mine, from_left, from_right))
    mine = jnp.broadcast_to(mine[None], (cols, share, SIZE))
    probe_grad = lax.all_to_all(mine, "col", split_axis=0, concat_axis=0, tiled=True)
    probe_grad = probe_grad.astype(F32).reshape(probe.shape)
    from_right = jnp.pad(from_right.astype(F32), ((0, 0), (0, 0), (0, 0), (HALF, 0)))
    return own_grad + from_left.astype(F32) + from_right, probe_grad


def solution(mesh):
    in_specs = (
        P(None, None, "row", "col"),
        P(),
        P(("row", "col"), None, None),
        P(),
        P(),
        P(("row", "col"), None),
        P(("row", "col"), None),
        P("row", "col"),
    )
    out_specs = (P(None, None, "row", "col"), P())
    return jax.shard_map(body, mesh=mesh, in_specs=in_specs, out_specs=out_specs, check_vma=False)
```

```python
import math

import jax
import jax.numpy as jnp
import numpy as np
from jax import lax
from jax.experimental import pallas as pl
from jax.experimental.pallas import tpu as pltpu
from jax.sharding import PartitionSpec as P

SIZE = 256
HALF = 128
MODES = 4
CHUNK = 32
SLOTS = 8
BF16 = jnp.bfloat16
F32 = jnp.float32


def dft_tables():
    index = np.arange(SIZE)
    phase = 2.0 * np.pi * ((index[:, None] * index[None, :]) % SIZE) / SIZE
    real = np.cos(phase) / math.sqrt(SIZE)
    imag = -np.sin(phase) / math.sqrt(SIZE)
    left = np.block([[real, -imag], [imag, real]])
    right = np.block([[real, imag], [-imag, real]])
    return jnp.asarray(left, F32).astype(BF16), jnp.asarray(right, F32).astype(BF16)


def describe_kernel(info, notes):
    tiles = notes.shape[0] // SLOTS
    scans = (info.shape[0] - 2) // 4
    level = [(info[2 * n] // HALF) % 4 for n in range(scans)]
    straddles = [(info[2 * n + 1] // HALF) % 2 for n in range(scans)]
    tile = [info[2 * scans + 2 * n] for n in range(scans)]
    live = [(n < info[4 * scans]).astype(jnp.int32) for n in range(scans)]
    zero = jnp.int32(0)
    before, after = [zero] * scans, [zero] * scans
    for two in range(scans):
        for one in range(two):
            same = (tile[one] == tile[two]) & (straddles[one] + straddles[two] == 2)
            same = same.astype(jnp.int32)
            before[two], after[one] = before[two] | same, after[one] | same
    owner = [tile[n] + before[n] for n in range(scans)]
    odd = info[4 * scans + 1]
    aside = 2 * odd - 1
    other = [
        lax.rem(tile[n] + straddles[n] + (1 - straddles[n]) * aside + tiles, tiles)
        for n in range(scans)
    ]
    for n in range(scans):
        free = live[n] * (1 - before[n]) * (1 - after[n])
        for k in range(scans):
            if k != n:
                free = free * (1 - (owner[k] == other[n]).astype(jnp.int32))
            if k < n:
                free = free * (1 - (other[k] == other[n]).astype(jnp.int32))
        column = (1 + straddles[n] - 2 * before[n] + odd) & 3
        moved_column = (3 * (1 - straddles[n]) + odd) & 3
        note = live[n] + 2 * free + 4 * owner[n] + 64 * other[n] + 1024 * level[n]
        note = note + 4096 * column + 16384 * moved_column
        for t in range(tiles):
            notes[t * SLOTS + n] = note
    for t in range(tiles):
        for n in range(scans, SLOTS):
            notes[t * SLOTS + n] = 0


def assign_kernel(me, notes, codes, homes, loads, moves):
    tiles = codes.shape[0]
    scans = homes.shape[0]
    for t in range(tiles):
        loads[t] = 0
        codes[t] = 0

    def fields(place):
        note = notes[place]
        return note & 1, (note >> 1) & 1, (note >> 2) & 15, (note >> 6) & 15, note

    @pl.loop(0, tiles)
    def _(source):
        for n in range(scans):
            live, _, owner, _, _ = fields(source * SLOTS + n)
            loads[owner] += live
            moves[source * SLOTS + n] = 0

    for _ in range(2):

        @pl.loop(0, tiles)
        def _(source):
            for n in range(scans):
                place = source * SLOTS + n
                _, free, owner, other, _ = fields(place)
                gain = (loads[owner] > loads[other] + 1).astype(jnp.int32)
                step = free * gain * (1 - moves[place])
                loads[owner] -= step
                loads[other] += step
                moves[place] += step

    @pl.loop(0, tiles)
    def _(source):
        code = jnp.int32(0)
        for n in range(scans):
            place = source * SLOTS + n
            live, _, owner, other, note = fields(place)
            moved = moves[place] == 1
            home = jnp.where(moved, other, owner)
            column = jnp.where(moved, (note >> 14) & 3, (note >> 12) & 3)
            here = live * (home == me[0]).astype(jnp.int32)
            code = code + here * (1 + 4 * ((note >> 10) & 3) + column)

            @pl.when(source == me[0])
            def _():
                homes[n] = jnp.where(live == 1, home, -1)

        codes[source] = code


def cast_kernel(odd, obj, tile_low, half):
    side = pl.multiple_of((1 - odd[0]) * HALF, HALF)
    tile_low[...] = obj[...].astype(BF16)
    half[...] = obj[:, :, :, pl.ds(side, HALF)].astype(BF16)


def pack_kernel(homes, measured, slots):
    for n in range(measured.shape[0]):

        @pl.when(homes[n] >= 0)
        def _():
            slots[homes[n]] = measured[n].astype(BF16)


def table_kernel(taps, tables, adjoints):
    def banded(row, shift):
        line = jnp.broadcast_to(taps[row : row + 1, :], (SIZE, 2 * SIZE))
        return pltpu.roll(line, shift, 1, stride=1, stride_axis=0)[:, :SIZE]

    straight, turned = 2 * SIZE - 32, 2 * SIZE - 31

    def put(out, real, imag, from_left):
        sign = 1.0 if from_left else -1.0
        out[:SIZE, :SIZE] = real.astype(BF16)
        out[:SIZE, SIZE:] = (-sign * imag).astype(BF16)
        out[SIZE:, :SIZE] = (sign * imag).astype(BF16)
        out[SIZE:, SIZE:] = real.astype(BF16)

    put(tables.at[0], banded(0, straight), banded(1, straight), True)
    put(tables.at[1], banded(6, turned), banded(7, turned), False)
    put(adjoints.at[0], banded(4, turned), -banded(5, turned), True)
    put(adjoints.at[1], banded(2, straight), -banded(3, straight), False)


CHUNKS = [slice(at, at + CHUNK) for at in range(0, SIZE, CHUNK)]


def left_stage(table, rows_in, cols_in):
    for m in range(MODES):
        both = jnp.dot(table, rows_in[m], preferred_element_type=F32)
        here = slice(m * SIZE, (m + 1) * SIZE)
        cols_in[here, :SIZE] = both[:SIZE].astype(BF16)
        cols_in[here, SIZE:] = both[SIZE:].astype(BF16)


def right_stage(table, cols_in, out):
    for m in range(MODES):
        here = slice(m * SIZE, (m + 1) * SIZE)
        out[here, :] = jnp.dot(cols_in[here, :], table, preferred_element_type=F32)


def put_rows(rows_in, m, at, real, imag):
    rows_in[m, at.start : at.stop, :] = real.astype(BF16)
    rows_in[m, SIZE + at.start : SIZE + at.stop, :] = imag.astype(BF16)


def pair(ref, m, at):
    here = slice(m * SIZE + at.start, m * SIZE + at.stop)
    return ref[here, :SIZE], ref[here, SIZE:]


def extend(odd, full, tile, half, ext):
    ext[4 * odd] = half[...]
    ext[1 + odd], ext[2 + odd] = tile[:, :, :, :HALF], tile[:, :, :, HALF:]
    ext[3 - 3 * odd], ext[4 - 3 * odd] = full[:, :, :, :HALF], full[:, :, :, HALF:]


def live_list(codes, order):
    def note(slot, found):
        live = codes[slot] > 0

        @pl.when(live)
        def _():
            order[found] = slot

        return found + live.astype(jnp.int32)

    return lax.fori_loop(0, codes.shape[0], note, jnp.int32(0))


def place_of(code):
    return (code - 1) % 4, pl.multiple_of(((code - 1) // 4) * HALF, HALF)


def pair_of(patch, s, at):
    return patch[s, at, :SIZE].astype(F32), patch[s, at, SIZE:].astype(F32)


def forward_kernel(
    odd, codes, full, tile, half, probe, tables, dft_left, dft_right,
    moved_all, far_all, root_all, patch_all,
    ext, rows_in, cols_in, moved_two, far_two, root_two, patch_two, order, sems,
):
    extend(odd[0], full, tile, half, ext)
    found = live_list(codes, order)
    wholes = (moved_all, far_all, root_all, patch_all)
    buffers = (moved_two, far_two, root_two, patch_two)

    def copies(i):
        two = lax.rem(i, 2)
        return [
            pltpu.make_async_copy(buffers[k].at[two], wholes[k].at[order[i]], sems.at[two, k])
            for k in range(4)
        ]

    @pl.loop(0, found)
    def _(i):
        two = lax.rem(i, 2)
        moved, far, root, patch = (buffer.at[two] for buffer in buffers)

        @pl.when(i >= 2)
        def _():
            for copy in copies(i - 2):
                copy.wait()

        column, start = place_of(codes[order[i]])
        for s in range(2):
            for part in range(2):
                for side in range(2):
                    low = part * SIZE + side * HALF
                    patch[s, :, low : low + HALF] = ext[column + side, s, part, pl.ds(start, SIZE), :]
        for at in CHUNKS:
            o_re, o_im = pair_of(patch, 0, at)
            for m in range(MODES):
                p_re, p_im = probe[m, 0, at, :].astype(F32), probe[m, 1, at, :].astype(F32)
                put_rows(rows_in, m, at, p_re * o_re - p_im * o_im, p_re * o_im + p_im * o_re)
        left_stage(tables[0], rows_in, cols_in)
        right_stage(tables[1], cols_in, moved)
        for at in CHUNKS:
            o_re, o_im = pair_of(patch, 1, at)
            for m in range(MODES):
                v_re, v_im = pair(moved, m, at)
                put_rows(rows_in, m, at, v_re * o_re - v_im * o_im, v_re * o_im + v_im * o_re)
        left_stage(dft_left[...], rows_in, cols_in)
        right_stage(dft_right[...], cols_in, far)
        for at in CHUNKS:
            power = jnp.ones((CHUNK, SIZE), F32)
            for m in range(MODES):
                f_re, f_im = pair(far, m, at)
                power = power + (f_re * f_re + f_im * f_im)
            root[at, :] = 1.0 / jnp.sqrt(power)
        for copy in copies(i):
            copy.start()

    for last in (2, 1):

        @pl.when(found >= last)
        def _():
            for copy in copies(found - last):
                copy.wait()


def backward_kernel(
    odd, codes, dft_left, dft_right, probe_all, adjoints_all,
    moved_all, far_all, root_all, patch_all, slots_all,
    own_grad, full_grad, half_grad, probe_grad,
    rows_in, cols_in, moved_two, far_two, root_two, patch_two, slots_two,
    probe, adjoints, acc, probe_acc, order, sems, once, ends,
):
    found = live_list(codes, order)
    wholes = (far_all, slots_all, root_all, moved_all, patch_all)
    buffers = (far_two, slots_two, root_two, moved_two, patch_two)
    tables = [
        pltpu.make_async_copy(probe_all, probe, once.at[0]),
        pltpu.make_async_copy(adjoints_all, adjoints, once.at[1]),
    ]

    def copies(i):
        two = lax.rem(i, 2)
        return [
            pltpu.make_async_copy(wholes[k].at[order[i]], buffers[k].at[two], sems.at[two, k])
            for k in range(5)
        ]

    @pl.when(found > 0)
    def _():
        for copy in copies(0) + tables:
            copy.start()

    acc[...] = jnp.zeros(acc.shape, F32)
    probe_acc[...] = jnp.zeros(probe_acc.shape, F32)

    def add_piece(s, at, column, start, g_re, g_im):
        rows = pl.ds(pl.multiple_of(start + at.start, CHUNK), CHUNK)
        for part, value in ((0, g_re), (1, g_im)):
            value = value.astype(BF16).astype(F32)
            for side in range(2):
                acc[column + side, s, part, rows, :] += value[:, side * HALF : (side + 1) * HALF]

    @pl.loop(0, found)
    def _(i):
        two = lax.rem(i, 2)
        far, slot, root, moved, patch = (buffer.at[two] for buffer in buffers)

        @pl.when(i + 1 < found)
        def _():
            for copy in copies(i + 1):
                copy.start()

        column, start = place_of(codes[order[i]])
        for copy in copies(i):
            copy.wait()
        for at in CHUNKS:
            factor = 1.0 - slot[at, :].astype(F32) * root[at, :]
            for m in range(MODES):
                f_re, f_im = pair(far, m, at)
                put_rows(rows_in, m, at, factor * f_re, factor * f_im)
        left_stage(dft_right[...], rows_in, cols_in)
        right_stage(dft_left[...], cols_in, far)
        for at in CHUNKS:
            o_re, o_im = pair_of(patch, 1, at)
            g_re = jnp.zeros((CHUNK, SIZE), F32)
            g_im = jnp.zeros((CHUNK, SIZE), F32)
            for m in range(MODES):
                a_re, a_im = pair(far, m, at)
                v_re, v_im = pair(moved, m, at)
                g_re = g_re + (v_re * a_re + v_im * a_im)
                g_im = g_im + (v_re * a_im - v_im * a_re)
                put_rows(rows_in, m, at, o_re * a_re + o_im * a_im, o_re * a_im - o_im * a_re)
            add_piece(1, at, column, start, g_re, g_im)

        @pl.when(i == 0)
        def _():
            for copy in tables:
                copy.wait()

        left_stage(adjoints[0], rows_in, cols_in)
        right_stage(adjoints[1], cols_in, moved)
        for at in CHUNKS:
            o_re, o_im = pair_of(patch, 0, at)
            g_re = jnp.zeros((CHUNK, SIZE), F32)
            g_im = jnp.zeros((CHUNK, SIZE), F32)
            for m in range(MODES):
                i_re, i_im = pair(moved, m, at)
                p_re, p_im = probe[m, 0, at, :].astype(F32), probe[m, 1, at, :].astype(F32)
                g_re = g_re + (p_re * i_re + p_im * i_im)
                g_im = g_im + (p_re * i_im - p_im * i_re)
                probe_acc[m, 0, at, :] += o_re * i_re + o_im * i_im
                probe_acc[m, 1, at, :] += o_re * i_im - o_im * i_re
            add_piece(0, at, column, start, g_re, g_im)

    leave = [
        pltpu.make_async_copy(
            acc.at[1 + side + odd[0]],
            own_grad.at[:, :, :, pl.ds(side * HALF, HALF)],
            ends.at[side],
        )
        for side in range(2)
    ]
    for copy in leave:
        copy.start()
    half_grad[...] = acc[4 * odd[0]].astype(BF16)
    full_grad[:, :, :, :HALF] = acc[3 - 3 * odd[0]].astype(BF16)
    full_grad[:, :, :, HALF:] = acc[4 - 3 * odd[0]].astype(BF16)
    probe_grad[...] = probe_acc[...].astype(BF16)
    for copy in leave:
        copy.wait()


def whole(count):
    return [pl.BlockSpec(memory_space=pltpu.VMEM) for _ in range(count)]


def scalars(count):
    return [pl.BlockSpec(memory_space=pltpu.SMEM) for _ in range(count)]


def body(object_slices, probe, measured, tap_row, tap_col, scan_corner, correlation, scan_count):
    cols = lax.axis_size("col")
    rows = lax.axis_size("row")
    band = object_slices.shape[2]
    part_shape = (2, 2, band, HALF)
    limit = pltpu.CompilerParams(vmem_limit_bytes=56 * 1024 * 1024)

    tile_shape = (2, 2, band, SIZE)
    scans = measured.shape[0]
    odd = (lax.axis_index("row") % 2).reshape(1)
    info = [scan_corner.reshape(-1), correlation.reshape(-1), scan_count.reshape(-1), odd]
    notes = pl.pallas_call(
        describe_kernel,
        out_shape=jax.ShapeDtypeStruct((cols * SLOTS,), jnp.int32),
        in_specs=scalars(1),
        out_specs=pl.BlockSpec(memory_space=pltpu.SMEM),
        compiler_params=limit,
    )(jnp.concatenate(info))
    notes, object_slices = lax.optimization_barrier((notes, object_slices))
    row_notes = lax.all_to_all(
        notes.reshape(cols, SLOTS), "col", split_axis=0, concat_axis=0, tiled=True
    )
    tile_low, half = pl.pallas_call(
        cast_kernel,
        out_shape=[
            jax.ShapeDtypeStruct(tile_shape, BF16),
            jax.ShapeDtypeStruct(part_shape, BF16),
        ],
        in_specs=scalars(1) + whole(1),
        out_specs=whole(2),
        compiler_params=limit,
    )(odd, object_slices)
    row_notes, tile_low, half = lax.optimization_barrier((row_notes, tile_low, half))

    def ring(step):
        pairs = []
        for r in range(rows):
            way = step if r % 2 == 0 else -step
            pairs += [(r * cols + c, r * cols + (c + way) % cols) for c in range(cols)]
        return pairs

    both = ("row", "col")
    full = lax.ppermute(tile_low, both, ring(-1))
    half = lax.ppermute(half, both, ring(1))
    codes, homes = pl.pallas_call(
        assign_kernel,
        out_shape=[
            jax.ShapeDtypeStruct((cols,), jnp.int32),
            jax.ShapeDtypeStruct((scans,), jnp.int32),
        ],
        in_specs=scalars(2),
        out_specs=scalars(2),
        scratch_shapes=[
            pltpu.SMEM((cols,), jnp.int32),
            pltpu.SMEM((cols * SLOTS,), jnp.int32),
        ],
        compiler_params=limit,
    )(lax.axis_index("col").reshape(1), row_notes.reshape(cols * SLOTS))
    slots = pl.pallas_call(
        pack_kernel,
        out_shape=jax.ShapeDtypeStruct((cols, SIZE, SIZE), BF16),
        in_specs=scalars(1) + whole(1),
        out_specs=pl.BlockSpec(memory_space=pltpu.VMEM),
        compiler_params=limit,
    )(homes, measured)
    arrived = lax.all_to_all(slots, "col", split_axis=0, concat_axis=0, tiled=True)

    taps = jnp.concatenate([tap_row, tap_col], axis=0)
    taps = jnp.concatenate([taps, taps[:, ::-1]], axis=0)
    taps = jnp.pad(taps, ((0, 0), (0, 2 * SIZE - taps.shape[1])))
    tables, adjoints = pl.pallas_call(
        table_kernel,
        out_shape=[jax.ShapeDtypeStruct((2, 2 * SIZE, 2 * SIZE), BF16) for _ in range(2)],
        in_specs=whole(1),
        out_specs=whole(2),
        compiler_params=limit,
    )(taps)
    dft_left, dft_right = dft_tables()

    def anywhere(count):
        return [pl.BlockSpec(memory_space=pl.ANY) for _ in range(count)]

    field_shape = (MODES * SIZE, 2 * SIZE)
    patch_shape = (2, SIZE, 2 * SIZE)
    work = [
        pltpu.VMEM((MODES, 2 * SIZE, SIZE), BF16),
        pltpu.VMEM(field_shape, BF16),
        pltpu.VMEM((2,) + field_shape, F32),
        pltpu.VMEM((2,) + field_shape, F32),
        pltpu.VMEM((2, SIZE, SIZE), F32),
        pltpu.VMEM((2,) + patch_shape, BF16),
    ]
    order = pltpu.SMEM((cols,), jnp.int32)
    moved_all, far_all, root_all, patch_all = pl.pallas_call(
        forward_kernel,
        out_shape=[
            jax.ShapeDtypeStruct((cols,) + field_shape, F32),
            jax.ShapeDtypeStruct((cols,) + field_shape, F32),
            jax.ShapeDtypeStruct((cols, SIZE, SIZE), F32),
            jax.ShapeDtypeStruct((cols,) + patch_shape, BF16),
        ],
        in_specs=scalars(2) + whole(7),
        out_specs=anywhere(4),
        scratch_shapes=[pltpu.VMEM((5,) + part_shape, BF16)]
        + work
        + [order, pltpu.SemaphoreType.DMA((2, 4))],
        cost_estimate=pl.CostEstimate(flops=40 * 10**9, bytes_accessed=10**7, transcendentals=0),
        compiler_params=limit,
    )(odd, codes, full, tile_low, half, probe, tables, dft_left, dft_right)
    own_grad, full_grad, half_grad, probe_part = pl.pallas_call(
        backward_kernel,
        out_shape=[
            jax.ShapeDtypeStruct(tile_shape, F32),
            jax.ShapeDtypeStruct(tile_shape, BF16),
            jax.ShapeDtypeStruct(part_shape, BF16),
            jax.ShapeDtypeStruct(probe.shape, BF16),
        ],
        in_specs=scalars(2) + whole(2) + anywhere(7),
        out_specs=anywhere(1) + whole(3),
        scratch_shapes=work
        + [
            pltpu.VMEM((2, SIZE, SIZE), BF16),
            pltpu.VMEM(probe.shape, BF16),
            pltpu.VMEM(adjoints.shape, BF16),
            pltpu.VMEM((5,) + part_shape, F32),
            pltpu.VMEM(probe.shape, F32),
            order,
            pltpu.SemaphoreType.DMA((2, 5)),
            pltpu.SemaphoreType.DMA((2,)),
            pltpu.SemaphoreType.DMA((2,)),
        ],
        compiler_params=limit,
    )(
        odd, codes, dft_left, dft_right, probe, adjoints,
        moved_all, far_all, root_all, patch_all, arrived,
    )

    full_grad = lax.ppermute(full_grad, both, ring(1))
    half_grad = lax.ppermute(half_grad, both, ring(-1))
    share = MODES * 2 * SIZE // cols
    mine = lax.all_to_all(
        probe_part.reshape(cols, share, SIZE), "col", split_axis=0, concat_axis=0, tiled=True
    )
    mine = jnp.sum(mine.astype(F32), axis=0).astype(BF16)
    mine = jnp.broadcast_to(mine[None], (rows, share, SIZE))
    mine = lax.all_to_all(mine, "row", split_axis=0, concat_axis=0, tiled=True)
    scale = 1.0 / math.sqrt(measured.shape[0] * cols * rows)
    mine = (jnp.sum(mine.astype(F32), axis=0) * scale).astype(BF16)
    mine, full_grad, half_grad = lax.optimization_barrier((mine, full_grad, half_grad))
    mine = jnp.broadcast_to(mine[None], (cols, share, SIZE))
    probe_grad = lax.all_to_all(mine, "col", split_axis=0, concat_axis=0, tiled=True)
    probe_grad = probe_grad.astype(F32).reshape(probe.shape)
    half_grad = half_grad.astype(F32)
    nothing = jnp.zeros_like(half_grad)
    odd = odd[0] == 1
    halo = [jnp.where(odd, half_grad, nothing), jnp.where(odd, nothing, half_grad)]
    return own_grad + full_grad.astype(F32) + jnp.concatenate(halo, axis=-1), probe_grad


def solution(mesh):
    in_specs = (
        P(None, None, "row", "col"),
        P(),
        P(("row", "col"), None, None),
        P(),
        P(),
        P(("row", "col"), None),
        P(("row", "col"), None),
        P("row", "col"),
    )
    out_specs = (P(None, None, "row", "col"), P())
    return jax.shard_map(body, mesh=mesh, in_specs=in_specs, out_specs=out_specs, check_vma=False)
```

```python
import math

import jax
import jax.numpy as jnp
import numpy as np
from jax import lax
from jax.experimental import pallas as pl
from jax.experimental.pallas import tpu as pltpu
from jax.sharding import PartitionSpec as P

SIZE = 256
HALF = 128
MODES = 4
CHUNK = 32
SLOTS = 8
BF16 = jnp.bfloat16
F32 = jnp.float32


def dft_tables():
    index = np.arange(SIZE)
    phase = 2.0 * np.pi * ((index[:, None] * index[None, :]) % SIZE) / SIZE
    real = np.cos(phase) / math.sqrt(SIZE)
    imag = -np.sin(phase) / math.sqrt(SIZE)
    left = np.block([[real, -imag], [imag, real]])
    right = np.block([[real, imag], [-imag, real]])
    return jnp.asarray(left, F32).astype(BF16), jnp.asarray(right, F32).astype(BF16)


def describe_kernel(info, notes):
    tiles = notes.shape[0] // SLOTS
    scans = (info.shape[0] - 2) // 4
    level = [(info[2 * n] // HALF) % 4 for n in range(scans)]
    straddles = [(info[2 * n + 1] // HALF) % 2 for n in range(scans)]
    tile = [info[2 * scans + 2 * n] for n in range(scans)]
    live = [(n < info[4 * scans]).astype(jnp.int32) for n in range(scans)]
    zero = jnp.int32(0)
    before, after = [zero] * scans, [zero] * scans
    for two in range(scans):
        for one in range(two):
            same = (tile[one] == tile[two]) & (straddles[one] + straddles[two] == 2)
            same = same.astype(jnp.int32)
            before[two], after[one] = before[two] | same, after[one] | same
    odd = info[4 * scans + 1]
    shift = [straddles[n] * jnp.where(odd == 1, 1 - after[n], before[n]) for n in range(scans)]
    owner = [tile[n] + shift[n] for n in range(scans)]
    aside = [jnp.where(straddles[n] == 1, 1 - shift[n], 2 * odd - 1) for n in range(scans)]
    other = [lax.rem(tile[n] + aside[n] + tiles, tiles) for n in range(scans)]
    for n in range(scans):
        free = live[n] * (1 - before[n]) * (1 - after[n])
        for k in range(scans):
            if k != n:
                free = free * (1 - (owner[k] == other[n]).astype(jnp.int32))
            if k < n:
                free = free * (1 - (other[k] == other[n]).astype(jnp.int32))
        column = (jnp.where(straddles[n] == 1, 2 - 2 * shift[n], 1) + odd) & 3
        moved_column = (jnp.where(straddles[n] == 1, 2 * shift[n], 3) + odd) & 3
        note = live[n] + 2 * free + 4 * owner[n] + 64 * other[n] + 1024 * level[n]
        note = note + 4096 * column + 16384 * moved_column
        for t in range(tiles):
            notes[t * SLOTS + n] = note
    for t in range(tiles):
        for n in range(scans, SLOTS):
            notes[t * SLOTS + n] = 0


def assign_kernel(me, notes, codes, homes, loads):
    tiles = codes.shape[0]
    scans = homes.shape[0]
    for t in range(tiles):
        loads[t] = 0

    @pl.loop(0, tiles)
    def _(source):
        for n in range(scans):
            note = notes[source * SLOTS + n]
            loads[(note >> 2) & 15] += note & 1

    @pl.loop(0, tiles)
    def _(source):
        code = jnp.int32(0)
        for n in range(scans):
            note = notes[source * SLOTS + n]
            owner, other = (note >> 2) & 15, (note >> 6) & 15
            here, there = loads[owner], loads[other]
            move = ((note >> 1) & 1) * (here > there + 1).astype(jnp.int32)
            loads[owner] = here - move
            loads[other] = loads[other] + move
            home = jnp.where(move == 1, other, owner)
            column = (note >> (12 + 2 * move)) & 3
            mine = (note & 1) * (home == me[0]).astype(jnp.int32)
            code = code + mine * (1 + 4 * ((note >> 10) & 3) + column)

            @pl.when(source == me[0])
            def _():
                homes[n] = jnp.where((note & 1) == 1, home, -1)

        codes[source] = code


def cast_kernel(odd, obj, tile_low, half):
    side = pl.multiple_of((1 - odd[0]) * HALF, HALF)
    tile_low[...] = obj[...].astype(BF16)
    half[...] = obj[:, :, :, pl.ds(side, HALF)].astype(BF16)


def pack_kernel(homes, measured, slots):
    for n in range(measured.shape[0]):

        @pl.when(homes[n] >= 0)
        def _():
            slots[homes[n]] = measured[n].astype(BF16)


def banded(taps, row, shift):
    line = jnp.broadcast_to(taps[row : row + 1, :], (SIZE, 2 * SIZE))
    return pltpu.roll(line, shift, 1, stride=1, stride_axis=0)[:, :SIZE]


STRAIGHT, TURNED = 2 * SIZE - 32, 2 * SIZE - 31


def put_table(out, real, imag, from_left):
    sign = 1.0 if from_left else -1.0
    out[:SIZE, :SIZE] = real.astype(BF16)
    out[:SIZE, SIZE:] = (-sign * imag).astype(BF16)
    out[SIZE:, :SIZE] = (sign * imag).astype(BF16)
    out[SIZE:, SIZE:] = real.astype(BF16)


def put_tables(taps, tables):
    put_table(tables.at[0], banded(taps, 0, STRAIGHT), banded(taps, 1, STRAIGHT), True)
    put_table(tables.at[1], banded(taps, 6, TURNED), banded(taps, 7, TURNED), False)


def put_adjoints(taps, tables):
    put_table(tables.at[0], banded(taps, 4, TURNED), -banded(taps, 5, TURNED), True)
    put_table(tables.at[1], banded(taps, 2, STRAIGHT), -banded(taps, 3, STRAIGHT), False)


CHUNKS = [slice(at, at + CHUNK) for at in range(0, SIZE, CHUNK)]


def left_stage(table, rows_in, cols_in):
    both = jnp.dot(table, rows_in[...], preferred_element_type=F32).astype(BF16)
    for m in range(MODES):
        rows, cols = slice(m * SIZE, (m + 1) * SIZE), slice(m * SIZE, (m + 1) * SIZE)
        cols_in[rows, :SIZE] = both[:SIZE, cols]
        cols_in[rows, SIZE:] = both[SIZE:, cols]


def right_stage(table, cols_in, out):
    out[...] = jnp.dot(cols_in[...], table, preferred_element_type=F32)


def put_rows(rows_in, m, at, real, imag):
    cols = slice(m * SIZE, (m + 1) * SIZE)
    rows_in[at.start : at.stop, cols] = real.astype(BF16)
    rows_in[SIZE + at.start : SIZE + at.stop, cols] = imag.astype(BF16)


def pair(ref, m, at):
    here = slice(m * SIZE + at.start, m * SIZE + at.stop)
    return ref[here, :SIZE], ref[here, SIZE:]


def extend(odd, full, tile, half, ext):
    ext[4 * odd] = half[...]
    ext[1 + odd], ext[2 + odd] = tile[:, :, :, :HALF], tile[:, :, :, HALF:]
    ext[3 - 3 * odd], ext[4 - 3 * odd] = full[:, :, :, :HALF], full[:, :, :, HALF:]


def live_list(codes, order):
    def note(slot, found):
        live = codes[slot] > 0

        @pl.when(live)
        def _():
            order[found] = slot

        return found + live.astype(jnp.int32)

    return lax.fori_loop(0, codes.shape[0], note, jnp.int32(0))


def place_of(code):
    return (code - 1) % 4, pl.multiple_of(((code - 1) // 4) * HALF, HALF)


def pair_of(patch, s, at):
    return patch[s, at, :SIZE].astype(F32), patch[s, at, SIZE:].astype(F32)


def forward_kernel(
    odd, codes, full, tile, half, probe, taps, dft_left, dft_right,
    moved_all, far_all, root_all, patch_all,
    ext, tables, rows_in, cols_in, moved_two, far_two, root_two, patch_two, order, sems,
):
    extend(odd[0], full, tile, half, ext)
    put_tables(taps, tables)
    found = live_list(codes, order)
    wholes = (moved_all, far_all, root_all, patch_all)
    buffers = (moved_two, far_two, root_two, patch_two)

    def copies(i):
        two = lax.rem(i, 2)
        return [
            pltpu.make_async_copy(buffers[k].at[two], wholes[k].at[order[i]], sems.at[two, k])
            for k in range(4)
        ]

    @pl.loop(0, found)
    def _(i):
        two = lax.rem(i, 2)
        moved, far, root, patch = (buffer.at[two] for buffer in buffers)

        @pl.when(i >= 2)
        def _():
            for copy in copies(i - 2):
                copy.wait()

        column, start = place_of(codes[order[i]])
        for s in range(2):
            for part in range(2):
                for side in range(2):
                    low = part * SIZE + side * HALF
                    patch[s, :, low : low + HALF] = ext[column + side, s, part, pl.ds(start, SIZE), :]
        for at in CHUNKS:
            o_re, o_im = pair_of(patch, 0, at)
            for m in range(MODES):
                p_re, p_im = probe[m, 0, at, :].astype(F32), probe[m, 1, at, :].astype(F32)
                put_rows(rows_in, m, at, p_re * o_re - p_im * o_im, p_re * o_im + p_im * o_re)
        left_stage(tables[0], rows_in, cols_in)
        right_stage(tables[1], cols_in, moved)
        for at in CHUNKS:
            o_re, o_im = pair_of(patch, 1, at)
            for m in range(MODES):
                v_re, v_im = pair(moved, m, at)
                put_rows(rows_in, m, at, v_re * o_re - v_im * o_im, v_re * o_im + v_im * o_re)
        left_stage(dft_left[...], rows_in, cols_in)
        right_stage(dft_right[...], cols_in, far)
        for at in CHUNKS:
            power = jnp.ones((CHUNK, SIZE), F32)
            for m in range(MODES):
                f_re, f_im = pair(far, m, at)
                power = power + (f_re * f_re + f_im * f_im)
            root[at, :] = 1.0 / jnp.sqrt(power)
        for copy in copies(i):
            copy.start()

    for last in (2, 1):

        @pl.when(found >= last)
        def _():
            for copy in copies(found - last):
                copy.wait()


def backward_kernel(
    odd, codes, dft_left, dft_right, taps, probe_all,
    moved_all, far_all, root_all, patch_all, slots_all,
    own_grad, full_grad, half_grad, probe_grad,
    rows_in, cols_in, moved_two, far_two, root_two, patch_two, slots_two,
    probe, adjoints, acc, probe_acc, order, sems, once, ends,
):
    found = live_list(codes, order)
    wholes = (far_all, slots_all, root_all, moved_all, patch_all)
    buffers = (far_two, slots_two, root_two, moved_two, patch_two)
    probe_copy = pltpu.make_async_copy(probe_all, probe, once)

    def copies(i):
        two = lax.rem(i, 2)
        return [
            pltpu.make_async_copy(wholes[k].at[order[i]], buffers[k].at[two], sems.at[two, k])
            for k in range(5)
        ]

    @pl.when(found > 0)
    def _():
        for copy in copies(0) + [probe_copy]:
            copy.start()

    put_adjoints(taps, adjoints)
    acc[...] = jnp.zeros(acc.shape, F32)
    probe_acc[...] = jnp.zeros(probe_acc.shape, F32)

    def add_piece(s, at, column, start, g_re, g_im):
        rows = pl.ds(pl.multiple_of(start + at.start, CHUNK), CHUNK)
        for part, value in ((0, g_re), (1, g_im)):
            value = value.astype(BF16).astype(F32)
            for side in range(2):
                acc[column + side, s, part, rows, :] += value[:, side * HALF : (side + 1) * HALF]

    @pl.loop(0, found)
    def _(i):
        two = lax.rem(i, 2)
        far, slot, root, moved, patch = (buffer.at[two] for buffer in buffers)

        @pl.when(i + 1 < found)
        def _():
            for copy in copies(i + 1):
                copy.start()

        column, start = place_of(codes[order[i]])
        for copy in copies(i):
            copy.wait()
        for at in CHUNKS:
            factor = 1.0 - slot[at, :].astype(F32) * root[at, :]
            for m in range(MODES):
                f_re, f_im = pair(far, m, at)
                put_rows(rows_in, m, at, factor * f_re, factor * f_im)
        left_stage(dft_right[...], rows_in, cols_in)
        right_stage(dft_left[...], cols_in, far)
        for at in CHUNKS:
            o_re, o_im = pair_of(patch, 1, at)
            g_re = jnp.zeros((CHUNK, SIZE), F32)
            g_im = jnp.zeros((CHUNK, SIZE), F32)
            for m in range(MODES):
                a_re, a_im = pair(far, m, at)
                v_re, v_im = pair(moved, m, at)
                g_re = g_re + (v_re * a_re + v_im * a_im)
                g_im = g_im + (v_re * a_im - v_im * a_re)
                put_rows(rows_in, m, at, o_re * a_re + o_im * a_im, o_re * a_im - o_im * a_re)
            add_piece(1, at, column, start, g_re, g_im)

        left_stage(adjoints[0], rows_in, cols_in)
        right_stage(adjoints[1], cols_in, moved)

        @pl.when(i == 0)
        def _():
            probe_copy.wait()

        for at in CHUNKS:
            o_re, o_im = pair_of(patch, 0, at)
            g_re = jnp.zeros((CHUNK, SIZE), F32)
            g_im = jnp.zeros((CHUNK, SIZE), F32)
            for m in range(MODES):
                i_re, i_im = pair(moved, m, at)
                p_re, p_im = probe[m, 0, at, :].astype(F32), probe[m, 1, at, :].astype(F32)
                g_re = g_re + (p_re * i_re + p_im * i_im)
                g_im = g_im + (p_re * i_im - p_im * i_re)
                probe_acc[m, 0, at, :] += o_re * i_re + o_im * i_im
                probe_acc[m, 1, at, :] += o_re * i_im - o_im * i_re
            add_piece(0, at, column, start, g_re, g_im)

    leave = [
        pltpu.make_async_copy(
            acc.at[1 + side + odd[0]],
            own_grad.at[:, :, :, pl.ds(side * HALF, HALF)],
            ends.at[side],
        )
        for side in range(2)
    ]
    for copy in leave:
        copy.start()
    half_grad[...] = acc[4 * odd[0]].astype(BF16)
    full_grad[:, :, :, :HALF] = acc[3 - 3 * odd[0]].astype(BF16)
    full_grad[:, :, :, HALF:] = acc[4 - 3 * odd[0]].astype(BF16)
    probe_grad[...] = probe_acc[...].astype(BF16)
    for copy in leave:
        copy.wait()


def whole(count):
    return [pl.BlockSpec(memory_space=pltpu.VMEM) for _ in range(count)]


def scalars(count):
    return [pl.BlockSpec(memory_space=pltpu.SMEM) for _ in range(count)]


def body(object_slices, probe, measured, tap_row, tap_col, scan_corner, correlation, scan_count):
    cols = lax.axis_size("col")
    rows = lax.axis_size("row")
    band = object_slices.shape[2]
    part_shape = (2, 2, band, HALF)
    limit = pltpu.CompilerParams(vmem_limit_bytes=56 * 1024 * 1024)

    tile_shape = (2, 2, band, SIZE)
    scans = measured.shape[0]
    odd = (lax.axis_index("row") % 2).reshape(1)
    info = [scan_corner.reshape(-1), correlation.reshape(-1), scan_count.reshape(-1), odd]
    notes = pl.pallas_call(
        describe_kernel,
        out_shape=jax.ShapeDtypeStruct((cols * SLOTS,), jnp.int32),
        in_specs=scalars(1),
        out_specs=pl.BlockSpec(memory_space=pltpu.SMEM),
        compiler_params=limit,
    )(jnp.concatenate(info))
    notes, object_slices = lax.optimization_barrier((notes, object_slices))
    row_notes = lax.all_to_all(
        notes.reshape(cols, SLOTS), "col", split_axis=0, concat_axis=0, tiled=True
    )
    tile_low, half = pl.pallas_call(
        cast_kernel,
        out_shape=[
            jax.ShapeDtypeStruct(tile_shape, BF16),
            jax.ShapeDtypeStruct(part_shape, BF16),
        ],
        in_specs=scalars(1) + whole(1),
        out_specs=whole(2),
        compiler_params=limit,
    )(odd, object_slices)
    row_notes, tile_low, half = lax.optimization_barrier((row_notes, tile_low, half))

    def ring(step):
        pairs = []
        for r in range(rows):
            way = step if r % 2 == 0 else -step
            pairs += [(r * cols + c, r * cols + (c + way) % cols) for c in range(cols)]
        return pairs

    both = ("row", "col")
    full = lax.ppermute(tile_low, both, ring(-1))
    half = lax.ppermute(half, both, ring(1))
    codes, homes = pl.pallas_call(
        assign_kernel,
        out_shape=[
            jax.ShapeDtypeStruct((cols,), jnp.int32),
            jax.ShapeDtypeStruct((scans,), jnp.int32),
        ],
        in_specs=scalars(2),
        out_specs=scalars(2),
        scratch_shapes=[pltpu.SMEM((cols,), jnp.int32)],
        compiler_params=limit,
    )(lax.axis_index("col").reshape(1), row_notes.reshape(cols * SLOTS))
    slots = pl.pallas_call(
        pack_kernel,
        out_shape=jax.ShapeDtypeStruct((cols, SIZE, SIZE), BF16),
        in_specs=scalars(1) + whole(1),
        out_specs=pl.BlockSpec(memory_space=pltpu.VMEM),
        compiler_params=limit,
    )(homes, measured)
    arrived = lax.all_to_all(slots, "col", split_axis=0, concat_axis=0, tiled=True)

    taps = jnp.concatenate([tap_row, tap_col], axis=0)
    taps = jnp.concatenate([taps, taps[:, ::-1]], axis=0)
    taps = jnp.pad(taps, ((0, 0), (0, 2 * SIZE - taps.shape[1])))
    dft_left, dft_right = dft_tables()

    def anywhere(count):
        return [pl.BlockSpec(memory_space=pl.ANY) for _ in range(count)]

    field_shape = (MODES * SIZE, 2 * SIZE)
    patch_shape = (2, SIZE, 2 * SIZE)
    pair_shape = (2, 2 * SIZE, 2 * SIZE)
    work = [
        pltpu.VMEM((2 * SIZE, MODES * SIZE), BF16),
        pltpu.VMEM(field_shape, BF16),
        pltpu.VMEM((2,) + field_shape, F32),
        pltpu.VMEM((2,) + field_shape, F32),
        pltpu.VMEM((2, SIZE, SIZE), F32),
        pltpu.VMEM((2,) + patch_shape, BF16),
    ]
    order = pltpu.SMEM((cols,), jnp.int32)
    moved_all, far_all, root_all, patch_all = pl.pallas_call(
        forward_kernel,
        out_shape=[
            jax.ShapeDtypeStruct((cols,) + field_shape, F32),
            jax.ShapeDtypeStruct((cols,) + field_shape, F32),
            jax.ShapeDtypeStruct((cols, SIZE, SIZE), F32),
            jax.ShapeDtypeStruct((cols,) + patch_shape, BF16),
        ],
        in_specs=scalars(2) + whole(7),
        out_specs=anywhere(4),
        scratch_shapes=[pltpu.VMEM((5,) + part_shape, BF16), pltpu.VMEM(pair_shape, BF16)]
        + work
        + [order, pltpu.SemaphoreType.DMA((2, 4))],
        cost_estimate=pl.CostEstimate(flops=40 * 10**9, bytes_accessed=10**7, transcendentals=0),
        compiler_params=limit,
    )(odd, codes, full, tile_low, half, probe, taps, dft_left, dft_right)
    own_grad, full_grad, half_grad, probe_part = pl.pallas_call(
        backward_kernel,
        out_shape=[
            jax.ShapeDtypeStruct(tile_shape, F32),
            jax.ShapeDtypeStruct(tile_shape, BF16),
            jax.ShapeDtypeStruct(part_shape, BF16),
            jax.ShapeDtypeStruct(probe.shape, BF16),
        ],
        in_specs=scalars(2) + whole(3) + anywhere(6),
        out_specs=anywhere(1) + whole(3),
        scratch_shapes=work
        + [
            pltpu.VMEM((2, SIZE, SIZE), BF16),
            pltpu.VMEM(probe.shape, BF16),
            pltpu.VMEM(pair_shape, BF16),
            pltpu.VMEM((5,) + part_shape, F32),
            pltpu.VMEM(probe.shape, F32),
            order,
            pltpu.SemaphoreType.DMA((2, 5)),
            pltpu.SemaphoreType.DMA,
            pltpu.SemaphoreType.DMA((2,)),
        ],
        compiler_params=limit,
    )(
        odd, codes, dft_left, dft_right, taps, probe,
        moved_all, far_all, root_all, patch_all, arrived,
    )

    full_grad = lax.ppermute(full_grad, both, ring(1))
    half_grad = lax.ppermute(half_grad, both, ring(-1))
    share = MODES * 2 * SIZE // cols
    mine = lax.all_to_all(
        probe_part.reshape(cols, share, SIZE), "col", split_axis=0, concat_axis=0, tiled=True
    )
    mine = jnp.sum(mine.astype(F32), axis=0).astype(BF16)
    mine = jnp.broadcast_to(mine[None], (rows, share, SIZE))
    mine = lax.all_to_all(mine, "row", split_axis=0, concat_axis=0, tiled=True)
    scale = 1.0 / math.sqrt(measured.shape[0] * cols * rows)
    mine = (jnp.sum(mine.astype(F32), axis=0) * scale).astype(BF16)
    mine, full_grad, half_grad = lax.optimization_barrier((mine, full_grad, half_grad))
    mine = jnp.broadcast_to(mine[None], (cols, share, SIZE))
    probe_grad = lax.all_to_all(mine, "col", split_axis=0, concat_axis=0, tiled=True)
    probe_grad = probe_grad.astype(F32).reshape(probe.shape)
    half_grad = half_grad.astype(F32)
    nothing = jnp.zeros_like(half_grad)
    odd = odd[0] == 1
    halo = [jnp.where(odd, half_grad, nothing), jnp.where(odd, nothing, half_grad)]
    return own_grad + full_grad.astype(F32) + jnp.concatenate(halo, axis=-1), probe_grad


def solution(mesh):
    in_specs = (
        P(None, None, "row", "col"),
        P(),
        P(("row", "col"), None, None),
        P(),
        P(),
        P(("row", "col"), None),
        P(("row", "col"), None),
        P("row", "col"),
    )
    out_specs = (P(None, None, "row", "col"), P())
    return jax.shard_map(body, mesh=mesh, in_specs=in_specs, out_specs=out_specs, check_vma=False)
```

```python
import math

import jax
import jax.numpy as jnp
import numpy as np
from jax import lax
from jax.experimental import pallas as pl
from jax.experimental.pallas import tpu as pltpu
from jax.sharding import PartitionSpec as P

SIZE = 256
HALF = 128
MODES = 4
CHUNK = 16
SLOTS = 8
BF16 = jnp.bfloat16
F32 = jnp.float32


def dft_tables():
    index = np.arange(SIZE)
    phase = 2.0 * np.pi * ((index[:, None] * index[None, :]) % SIZE) / SIZE
    real = np.cos(phase) / math.sqrt(SIZE)
    imag = -np.sin(phase) / math.sqrt(SIZE)
    halves = []
    for first in range(2):
        re, im = real[first::2, :HALF], imag[first::2, :HALF]
        halves.append(np.block([[re, -im], [im, re]]))
    both = np.stack(halves + [half.T for half in halves])
    return jnp.asarray(both, F32).astype(BF16)


def sorter():
    index = np.arange(SIZE)
    place = index // 2 + HALF * (index % 2)
    sort = place[:, None] == index[None, :]
    return jnp.asarray(np.stack([sort, sort.T]), BF16)


def describe_kernel(info, notes):
    tiles = notes.shape[0] // SLOTS
    scans = (info.shape[0] - 2) // 4
    level = [(info[2 * n] // HALF) % 4 for n in range(scans)]
    straddles = [(info[2 * n + 1] // HALF) % 2 for n in range(scans)]
    tile = [info[2 * scans + 2 * n] for n in range(scans)]
    live = [(n < info[4 * scans]).astype(jnp.int32) for n in range(scans)]
    zero = jnp.int32(0)
    before, after = [zero] * scans, [zero] * scans
    for two in range(scans):
        for one in range(two):
            same = (tile[one] == tile[two]) & (straddles[one] + straddles[two] == 2)
            same = same.astype(jnp.int32)
            before[two], after[one] = before[two] | same, after[one] | same
    odd = info[4 * scans + 1]
    shift = [straddles[n] * jnp.where(odd == 1, 1 - after[n], before[n]) for n in range(scans)]
    owner = [tile[n] + shift[n] for n in range(scans)]
    aside = [jnp.where(straddles[n] == 1, 1 - shift[n], 2 * odd - 1) for n in range(scans)]
    other = [lax.rem(tile[n] + aside[n] + tiles, tiles) for n in range(scans)]
    for n in range(scans):
        free = live[n] * (1 - before[n]) * (1 - after[n])
        for k in range(scans):
            if k != n:
                free = free * (1 - (owner[k] == other[n]).astype(jnp.int32))
            if k < n:
                free = free * (1 - (other[k] == other[n]).astype(jnp.int32))
        column = (jnp.where(straddles[n] == 1, 2 - 2 * shift[n], 1) + odd) & 3
        moved_column = (jnp.where(straddles[n] == 1, 2 * shift[n], 3) + odd) & 3
        note = live[n] + 2 * free + 4 * owner[n] + 64 * other[n] + 1024 * level[n]
        note = note + 4096 * column + 16384 * moved_column
        for t in range(tiles):
            notes[t * SLOTS + n] = note
    for t in range(tiles):
        for n in range(scans, SLOTS):
            notes[t * SLOTS + n] = 0


def assign_kernel(me, notes, packed, codes, slots, loads, homes, sems):
    tiles = codes.shape[0]
    scans = packed.shape[0]
    for t in range(tiles):
        loads[t] = 0

    @pl.loop(0, tiles)
    def _(source):
        for n in range(scans):
            note = notes[source * SLOTS + n]
            loads[(note >> 2) & 15] += note & 1

    @pl.loop(0, tiles)
    def _(source):
        code = jnp.int32(0)
        for n in range(scans):
            note = notes[source * SLOTS + n]
            owner, other = (note >> 2) & 15, (note >> 6) & 15
            here, there = loads[owner], loads[other]
            move = ((note >> 1) & 1) * (here > there + 1).astype(jnp.int32)
            loads[owner] = here - move
            loads[other] = loads[other] + move
            home = jnp.where(move == 1, other, owner)
            column = (note >> (12 + 2 * move)) & 3
            mine = (note & 1) * (home == me[0]).astype(jnp.int32)
            code = code + mine * (1 + 4 * ((note >> 10) & 3) + column)

            @pl.when(source == me[0])
            def _():
                homes[n] = jnp.where((note & 1) == 1, home, -1)

        codes[source] = code

    def each(act):
        for n in range(scans):

            @pl.when(homes[n] >= 0)
            def _():
                act(pltpu.make_async_copy(packed.at[n], slots.at[homes[n]], sems.at[n]))

    each(lambda copy: copy.start())
    each(lambda copy: copy.wait())


def cast_kernel(odd, obj, tile_low, half):
    side = pl.multiple_of((1 - odd[0]) * HALF, HALF)
    tile_low[...] = obj[...].astype(BF16)
    half[...] = obj[:, :, :, pl.ds(side, HALF)].astype(BF16)


def sort_kernel(info, measured, sort, packed):
    scans = measured.shape[0]
    for n in range(scans):

        @pl.when(n < info[4 * scans])
        def _():
            rows = jnp.dot(sort[1], measured[n].astype(BF16), preferred_element_type=F32)
            both = jnp.dot(rows.astype(BF16), sort[0], preferred_element_type=F32)
            packed[n] = both.astype(BF16)


def banded(taps, row, shift):
    line = jnp.broadcast_to(taps[row : row + 1, :], (SIZE, 2 * SIZE))
    return pltpu.roll(line, shift, 1, stride=1, stride_axis=0)[:, :SIZE]


STRAIGHT, TURNED = 2 * SIZE - 32, 2 * SIZE - 31


def put_table(out, real, imag, from_left):
    sign = 1.0 if from_left else -1.0
    out[:SIZE, :SIZE] = real.astype(BF16)
    out[:SIZE, SIZE:] = (-sign * imag).astype(BF16)
    out[SIZE:, :SIZE] = (sign * imag).astype(BF16)
    out[SIZE:, SIZE:] = real.astype(BF16)


def put_tables(taps, tables):
    put_table(tables.at[0], banded(taps, 0, STRAIGHT), banded(taps, 1, STRAIGHT), True)
    put_table(tables.at[1], banded(taps, 6, TURNED), banded(taps, 7, TURNED), False)


def put_adjoints(taps, tables):
    put_table(tables.at[0], banded(taps, 4, TURNED), -banded(taps, 5, TURNED), True)
    put_table(tables.at[1], banded(taps, 2, STRAIGHT), -banded(taps, 3, STRAIGHT), False)


CHUNKS = [slice(at, at + CHUNK) for at in range(0, SIZE, CHUNK)]


def in_turn(*stages):
    for step in range(MODES + len(stages) - 1):
        for place, stage in enumerate(stages):
            if 0 <= step - place < MODES:
                stage(step - place)


def rows_of(m):
    return slice(m * SIZE, (m + 1) * SIZE)


def left_stage(table, rows_in, cols_in):
    def stage(m):
        both = jnp.dot(table, rows_in[m], preferred_element_type=F32)
        cols_in[rows_of(m), :SIZE] = both[:SIZE].astype(BF16)
        cols_in[rows_of(m), SIZE:] = both[SIZE:].astype(BF16)

    return stage


def right_stage(table, cols_in, out):
    def stage(m):
        out[rows_of(m), :] = jnp.dot(cols_in[rows_of(m), :], table, preferred_element_type=F32)

    return stage


def put_rows(rows_in, m, at, real, imag):
    rows_in[m, at.start : at.stop, :] = real.astype(BF16)
    rows_in[m, SIZE + at.start : SIZE + at.stop, :] = imag.astype(BF16)


def put_halves(rows_in, m, at, first, second):
    for place, part in enumerate(first + second):
        low = place * HALF + at.start
        rows_in[m, low : low + CHUNK, :] = part.astype(BF16)


def dft_left(dft, rows_in, cols_in):
    def stage(m):
        for first in range(2):
            part = slice(first * SIZE, (first + 1) * SIZE)
            both = jnp.dot(dft[first], rows_in[m, part, :], preferred_element_type=F32)
            rows = slice(m * SIZE + first * HALF, m * SIZE + (first + 1) * HALF)
            for k in range(2):
                here = both[k * HALF : (k + 1) * HALF]
                low, high = here[:, :HALF], here[:, HALF:]
                cols_in[rows, k * HALF : (k + 1) * HALF] = (low + high).astype(BF16)
                cols_in[rows, SIZE + k * HALF : SIZE + (k + 1) * HALF] = (low - high).astype(BF16)

    return stage


def dft_right(dft, cols_in, out):
    def stage(m):
        for first in range(2):
            part = slice(first * SIZE, (first + 1) * SIZE)
            both = jnp.dot(cols_in[rows_of(m), part], dft[2 + first], preferred_element_type=F32)
            for k in range(2):
                low = k * SIZE + first * HALF
                out[rows_of(m), low : low + HALF] = both[:, k * HALF : (k + 1) * HALF]

    return stage


def inverse_left(dft, rows_in, cols_in):
    def stage(m):
        even = jnp.dot(dft[2], rows_in[m, :SIZE, :], preferred_element_type=F32)
        odd = jnp.dot(dft[3], rows_in[m, SIZE:, :], preferred_element_type=F32)
        for k in range(2):
            part = slice(k * HALF, (k + 1) * HALF)
            sums = (even[part] + odd[part]).astype(BF16)
            gaps = (even[part] - odd[part]).astype(BF16)
            for side in range(2):
                here = slice(side * HALF, (side + 1) * HALF)
                low = side * SIZE + k * HALF
                cols_in[m * SIZE : m * SIZE + HALF, low : low + HALF] = sums[:, here]
                cols_in[m * SIZE + HALF : (m + 1) * SIZE, low : low + HALF] = gaps[:, here]

    return stage


def inverse_right(dft, cols_in, out):
    def stage(m):
        even = jnp.dot(cols_in[rows_of(m), :SIZE], dft[0], preferred_element_type=F32)
        odd = jnp.dot(cols_in[rows_of(m), SIZE:], dft[1], preferred_element_type=F32)
        for k in range(2):
            part = slice(k * HALF, (k + 1) * HALF)
            out[rows_of(m), k * SIZE : k * SIZE + HALF] = even[:, part] + odd[:, part]
            out[rows_of(m), k * SIZE + HALF : (k + 1) * SIZE] = even[:, part] - odd[:, part]

    return stage


def pair(ref, m, at):
    here = slice(m * SIZE + at.start, m * SIZE + at.stop)
    return ref[here, :SIZE], ref[here, SIZE:]


def extend(odd, full, tile, half, ext):
    ext[4 * odd] = half[...]
    ext[1 + odd], ext[2 + odd] = tile[:, :, :, :HALF], tile[:, :, :, HALF:]
    ext[3 - 3 * odd], ext[4 - 3 * odd] = full[:, :, :, :HALF], full[:, :, :, HALF:]


def live_list(codes, order):
    def note(slot, found):
        live = codes[slot] > 0

        @pl.when(live)
        def _():
            order[found] = slot

        return found + live.astype(jnp.int32)

    return lax.fori_loop(0, codes.shape[0], note, jnp.int32(0))


def place_of(code):
    return (code - 1) % 4, pl.multiple_of(((code - 1) // 4) * HALF, HALF)


def pair_of(patch, s, at):
    return patch[s, at, :SIZE].astype(F32), patch[s, at, SIZE:].astype(F32)


def forward_kernel(
    odd, codes, full, tile, half, probe, taps, dft,
    moved_all, far_all, root_all, patch_all,
    ext, tables, rows_in, cols_in, moved_two, far_two, root_two, patch_two, order, sems,
):
    extend(odd[0], full, tile, half, ext)
    put_tables(taps, tables)
    found = live_list(codes, order)
    wholes = (moved_all, far_all, root_all, patch_all)
    buffers = (moved_two, far_two, root_two, patch_two)

    def copies(i):
        two = lax.rem(i, 2)
        return [
            pltpu.make_async_copy(buffers[k].at[two], wholes[k].at[order[i]], sems.at[two, k])
            for k in range(4)
        ]

    @pl.loop(0, found)
    def _(i):
        two = lax.rem(i, 2)
        moved, far, root, patch = (buffer.at[two] for buffer in buffers)

        @pl.when(i >= 2)
        def _():
            for copy in copies(i - 2):
                copy.wait()

        column, start = place_of(codes[order[i]])
        for s in range(2):
            for part in range(2):
                for side in range(2):
                    low = part * SIZE + side * HALF
                    patch[s, :, low : low + HALF] = ext[column + side, s, part, pl.ds(start, SIZE), :]

        def wave(m):
            for at in CHUNKS:
                o_re, o_im = pair_of(patch, 0, at)
                p_re, p_im = probe[m, 0, at, :].astype(F32), probe[m, 1, at, :].astype(F32)
                put_rows(rows_in, m, at, p_re * o_re - p_im * o_im, p_re * o_im + p_im * o_re)

        def exit_wave(m):
            for at in CHUNKS[: len(CHUNKS) // 2]:
                down = slice(at.start + HALF, at.stop + HALF)
                o_re, o_im = pair_of(patch, 1, at)
                q_re, q_im = pair_of(patch, 1, down)
                v_re, v_im = pair(moved, m, at)
                w_re, w_im = pair(moved, m, down)
                a_re, a_im = v_re * o_re - v_im * o_im, v_re * o_im + v_im * o_re
                b_re, b_im = w_re * q_re - w_im * q_im, w_re * q_im + w_im * q_re
                put_halves(rows_in, m, at, (a_re + b_re, a_im + b_im), (a_re - b_re, a_im - b_im))

        in_turn(
            wave,
            left_stage(tables[0], rows_in, cols_in),
            right_stage(tables[1], cols_in, moved),
            exit_wave,
            dft_left(dft, rows_in, cols_in),
            dft_right(dft, cols_in, far),
        )
        for at in CHUNKS:
            power = jnp.ones((CHUNK, SIZE), F32)
            for m in range(MODES):
                f_re, f_im = pair(far, m, at)
                power = power + (f_re * f_re + f_im * f_im)
            root[at, :] = 1.0 / jnp.sqrt(power)
        for copy in copies(i):
            copy.start()

    for last in (2, 1):

        @pl.when(found >= last)
        def _():
            for copy in copies(found - last):
                copy.wait()


def backward_kernel(
    odd, codes, dft, taps, probe_all,
    moved_all, far_all, root_all, patch_all, slots_all,
    own_grad, full_grad, half_grad, probe_grad,
    rows_in, cols_in, moved_two, far_two, root_two, patch_two, slots_two,
    factor, probe, adjoints, acc, probe_acc, order, sems, once, ends,
):
    found = live_list(codes, order)
    wholes = (far_all, slots_all, root_all, moved_all, patch_all)
    buffers = (far_two, slots_two, root_two, moved_two, patch_two)
    probe_copy = pltpu.make_async_copy(probe_all, probe, once)

    def copies(i):
        two = lax.rem(i, 2)
        return [
            pltpu.make_async_copy(wholes[k].at[order[i]], buffers[k].at[two], sems.at[two, k])
            for k in range(5)
        ]

    @pl.when(found > 0)
    def _():
        for copy in copies(0) + [probe_copy]:
            copy.start()

    put_adjoints(taps, adjoints)
    acc[...] = jnp.zeros(acc.shape, F32)
    probe_acc[...] = jnp.zeros(probe_acc.shape, F32)

    def add_piece(s, at, column, start, g_re, g_im):
        rows = pl.ds(pl.multiple_of(start + at.start, CHUNK), CHUNK)
        for part, value in ((0, g_re), (1, g_im)):
            value = value.astype(BF16).astype(F32)
            for side in range(2):
                acc[column + side, s, part, rows, :] += value[:, side * HALF : (side + 1) * HALF]

    @pl.loop(0, found)
    def _(i):
        two = lax.rem(i, 2)
        far, slot, root, moved, patch = (buffer.at[two] for buffer in buffers)

        @pl.when(i + 1 < found)
        def _():
            for copy in copies(i + 1):
                copy.start()

        column, start = place_of(codes[order[i]])
        for copy in copies(i):
            copy.wait()

        def scaled(m):
            for at in CHUNKS[: len(CHUNKS) // 2]:
                down = slice(at.start + HALF, at.stop + HALF)
                f_re, f_im = pair(far, m, at)
                g_re, g_im = pair(far, m, down)
                top, low = factor[at, :], factor[down, :]
                put_halves(rows_in, m, at, (top * f_re, top * f_im), (low * g_re, low * g_im))

        for at in CHUNKS:
            factor[at, :] = 1.0 - slot[at, :].astype(F32) * root[at, :]
        in_turn(
            scaled,
            inverse_left(dft, rows_in, cols_in),
            inverse_right(dft, cols_in, far),
        )
        for at in CHUNKS:
            o_re, o_im = pair_of(patch, 1, at)
            g_re = jnp.zeros((CHUNK, SIZE), F32)
            g_im = jnp.zeros((CHUNK, SIZE), F32)
            for m in range(MODES):
                a_re, a_im = pair(far, m, at)
                v_re, v_im = pair(moved, m, at)
                g_re = g_re + (v_re * a_re + v_im * a_im)
                g_im = g_im + (v_re * a_im - v_im * a_re)
                put_rows(rows_in, m, at, o_re * a_re + o_im * a_im, o_re * a_im - o_im * a_re)
            add_piece(1, at, column, start, g_re, g_im)

        in_turn(
            left_stage(adjoints[0], rows_in, cols_in),
            right_stage(adjoints[1], cols_in, moved),
        )

        @pl.when(i == 0)
        def _():
            probe_copy.wait()

        for at in CHUNKS:
            o_re, o_im = pair_of(patch, 0, at)
            g_re = jnp.zeros((CHUNK, SIZE), F32)
            g_im = jnp.zeros((CHUNK, SIZE), F32)
            for m in range(MODES):
                i_re, i_im = pair(moved, m, at)
                p_re, p_im = probe[m, 0, at, :].astype(F32), probe[m, 1, at, :].astype(F32)
                g_re = g_re + (p_re * i_re + p_im * i_im)
                g_im = g_im + (p_re * i_im - p_im * i_re)
                probe_acc[m, 0, at, :] += o_re * i_re + o_im * i_im
                probe_acc[m, 1, at, :] += o_re * i_im - o_im * i_re
            add_piece(0, at, column, start, g_re, g_im)

    leave = [
        pltpu.make_async_copy(
            acc.at[1 + side + odd[0]],
            own_grad.at[:, :, :, pl.ds(side * HALF, HALF)],
            ends.at[side],
        )
        for side in range(2)
    ]
    for copy in leave:
        copy.start()
    half_grad[...] = acc[4 * odd[0]].astype(BF16)
    full_grad[:, :, :, :HALF] = acc[3 - 3 * odd[0]].astype(BF16)
    full_grad[:, :, :, HALF:] = acc[4 - 3 * odd[0]].astype(BF16)
    probe_grad[...] = probe_acc[...].astype(BF16)
    for copy in leave:
        copy.wait()


def whole(count):
    return [pl.BlockSpec(memory_space=pltpu.VMEM) for _ in range(count)]


def scalars(count):
    return [pl.BlockSpec(memory_space=pltpu.SMEM) for _ in range(count)]


def body(object_slices, probe, measured, tap_row, tap_col, scan_corner, correlation, scan_count):
    cols = lax.axis_size("col")
    rows = lax.axis_size("row")
    band = object_slices.shape[2]
    part_shape = (2, 2, band, HALF)
    limit = pltpu.CompilerParams(vmem_limit_bytes=56 * 1024 * 1024)

    tile_shape = (2, 2, band, SIZE)
    scans = measured.shape[0]
    odd = (lax.axis_index("row") % 2).reshape(1)
    def anywhere(count):
        return [pl.BlockSpec(memory_space=pl.ANY) for _ in range(count)]

    def ring(step):
        pairs = []
        for r in range(rows):
            way = step if r % 2 == 0 else -step
            pairs += [(r * cols + c, r * cols + (c + way) % cols) for c in range(cols)]
        return pairs

    both = ("row", "col")
    tile_low, half = pl.pallas_call(
        cast_kernel,
        out_shape=[
            jax.ShapeDtypeStruct(tile_shape, BF16),
            jax.ShapeDtypeStruct(part_shape, BF16),
        ],
        in_specs=scalars(1) + whole(1),
        out_specs=whole(2),
        compiler_params=limit,
    )(odd, object_slices)
    full = lax.ppermute(tile_low, both, ring(-1))
    half = lax.ppermute(half, both, ring(1))

    info = [scan_corner.reshape(-1), correlation.reshape(-1), scan_count.reshape(-1), odd]
    info = jnp.concatenate(info)
    notes = pl.pallas_call(
        describe_kernel,
        out_shape=jax.ShapeDtypeStruct((cols * SLOTS,), jnp.int32),
        in_specs=scalars(1),
        out_specs=pl.BlockSpec(memory_space=pltpu.SMEM),
        compiler_params=limit,
    )(info)
    row_notes = lax.all_to_all(
        notes.reshape(cols, SLOTS), "col", split_axis=0, concat_axis=0, tiled=True
    )
    packed = pl.pallas_call(
        sort_kernel,
        out_shape=jax.ShapeDtypeStruct((scans, SIZE, SIZE), BF16),
        in_specs=scalars(1) + whole(2),
        out_specs=pl.BlockSpec(memory_space=pltpu.VMEM),
        compiler_params=limit,
    )(info, measured, sorter())
    codes, slots = pl.pallas_call(
        assign_kernel,
        out_shape=[
            jax.ShapeDtypeStruct((cols,), jnp.int32),
            jax.ShapeDtypeStruct((cols, SIZE, SIZE), BF16),
        ],
        in_specs=scalars(2) + whole(1),
        out_specs=scalars(1) + anywhere(1),
        scratch_shapes=[
            pltpu.SMEM((cols,), jnp.int32),
            pltpu.SMEM((scans,), jnp.int32),
            pltpu.SemaphoreType.DMA((scans,)),
        ],
        compiler_params=limit,
    )(lax.axis_index("col").reshape(1), row_notes.reshape(cols * SLOTS), packed)
    arrived = lax.all_to_all(slots, "col", split_axis=0, concat_axis=0, tiled=True)

    taps = jnp.concatenate([tap_row, tap_col], axis=0)
    taps = jnp.concatenate([taps, taps[:, ::-1]], axis=0)
    taps = jnp.pad(taps, ((0, 0), (0, 2 * SIZE - taps.shape[1])))
    dft = dft_tables()

    field_shape = (MODES * SIZE, 2 * SIZE)
    patch_shape = (2, SIZE, 2 * SIZE)
    pair_shape = (2, 2 * SIZE, 2 * SIZE)
    work = [
        pltpu.VMEM((MODES, 2 * SIZE, SIZE), BF16),
        pltpu.VMEM(field_shape, BF16),
        pltpu.VMEM((2,) + field_shape, F32),
        pltpu.VMEM((2,) + field_shape, F32),
        pltpu.VMEM((2, SIZE, SIZE), F32),
        pltpu.VMEM((2,) + patch_shape, BF16),
    ]
    order = pltpu.SMEM((cols,), jnp.int32)
    moved_all, far_all, root_all, patch_all = pl.pallas_call(
        forward_kernel,
        out_shape=[
            jax.ShapeDtypeStruct((cols,) + field_shape, F32),
            jax.ShapeDtypeStruct((cols,) + field_shape, F32),
            jax.ShapeDtypeStruct((cols, SIZE, SIZE), F32),
            jax.ShapeDtypeStruct((cols,) + patch_shape, BF16),
        ],
        in_specs=scalars(2) + whole(6),
        out_specs=anywhere(4),
        scratch_shapes=[pltpu.VMEM((5,) + part_shape, BF16), pltpu.VMEM(pair_shape, BF16)]
        + work
        + [order, pltpu.SemaphoreType.DMA((2, 4))],
        cost_estimate=pl.CostEstimate(flops=40 * 10**9, bytes_accessed=10**7, transcendentals=0),
        compiler_params=limit,
    )(odd, codes, full, tile_low, half, probe, taps, dft)
    own_grad, full_grad, half_grad, probe_part = pl.pallas_call(
        backward_kernel,
        out_shape=[
            jax.ShapeDtypeStruct(tile_shape, F32),
            jax.ShapeDtypeStruct(tile_shape, BF16),
            jax.ShapeDtypeStruct(part_shape, BF16),
            jax.ShapeDtypeStruct(probe.shape, BF16),
        ],
        in_specs=scalars(2) + whole(2) + anywhere(6),
        out_specs=anywhere(1) + whole(3),
        scratch_shapes=work
        + [
            pltpu.VMEM((2, SIZE, SIZE), BF16),
            pltpu.VMEM((SIZE, SIZE), F32),
            pltpu.VMEM(probe.shape, BF16),
            pltpu.VMEM(pair_shape, BF16),
            pltpu.VMEM((5,) + part_shape, F32),
            pltpu.VMEM(probe.shape, F32),
            order,
            pltpu.SemaphoreType.DMA((2, 5)),
            pltpu.SemaphoreType.DMA,
            pltpu.SemaphoreType.DMA((2,)),
        ],
        compiler_params=limit,
    )(
        odd, codes, dft, taps, probe,
        moved_all, far_all, root_all, patch_all, arrived,
    )

    full_grad = lax.ppermute(full_grad, both, ring(1))
    half_grad = lax.ppermute(half_grad, both, ring(-1))
    lines = MODES * 2 * SIZE // rows
    share = lines // cols

    def swap(blocks, axis):
        return lax.all_to_all(blocks, axis, split_axis=0, concat_axis=0, tiled=True)

    mine = swap(probe_part.reshape(rows, lines, SIZE), "row")
    mine = jnp.sum(mine.astype(F32), axis=0).astype(BF16)
    mine = swap(mine.reshape(cols, share, SIZE), "col")
    scale = 1.0 / math.sqrt(scans * cols * rows)
    mine = (jnp.sum(mine.astype(F32), axis=0) * scale).astype(BF16)
    mine = swap(jnp.broadcast_to(mine[None], (cols, share, SIZE)), "col")
    mine, full_grad, half_grad = lax.optimization_barrier((mine, full_grad, half_grad))
    mine = mine.reshape(lines, SIZE)
    probe_grad = swap(jnp.broadcast_to(mine[None], (rows, lines, SIZE)), "row")
    probe_grad = probe_grad.astype(F32).reshape(probe.shape)
    half_grad = half_grad.astype(F32)
    nothing = jnp.zeros_like(half_grad)
    odd = odd[0] == 1
    halo = [jnp.where(odd, half_grad, nothing), jnp.where(odd, nothing, half_grad)]
    return own_grad + full_grad.astype(F32) + jnp.concatenate(halo, axis=-1), probe_grad


def solution(mesh):
    in_specs = (
        P(None, None, "row", "col"),
        P(),
        P(("row", "col"), None, None),
        P(),
        P(),
        P(("row", "col"), None),
        P(("row", "col"), None),
        P("row", "col"),
    )
    out_specs = (P(None, None, "row", "col"), P())
    return jax.shard_map(body, mesh=mesh, in_specs=in_specs, out_specs=out_specs, check_vma=False)
```

```python
import math

import jax
import jax.numpy as jnp
import numpy as np
from jax import lax
from jax.experimental import pallas as pl
from jax.experimental.pallas import tpu as pltpu
from jax.sharding import PartitionSpec as P

SIZE = 256
HALF = 128
MODES = 4
CHUNK = 16
SLOTS = 8
BF16 = jnp.bfloat16
F32 = jnp.float32


def dft_tables():
    index = np.arange(SIZE)
    phase = 2.0 * np.pi * ((index[:, None] * index[None, :]) % SIZE) / SIZE
    real = np.cos(phase) / math.sqrt(SIZE)
    imag = -np.sin(phase) / math.sqrt(SIZE)
    halves = []
    for first in range(2):
        re, im = real[first::2, :HALF], imag[first::2, :HALF]
        halves.append(np.block([[re, -im], [im, re]]))
    both = np.stack(halves + [half.T for half in halves])
    return jnp.asarray(both, F32).astype(BF16)


def sorter():
    index = np.arange(SIZE)
    place = index // 2 + HALF * (index % 2)
    sort = place[:, None] == index[None, :]
    return jnp.asarray(np.stack([sort, sort.T]), BF16)


def describe_kernel(info, notes):
    tiles = notes.shape[0]
    scans = (info.shape[0] - 2) // 4
    level = [(info[2 * n] // HALF) % 4 for n in range(scans)]
    straddles = [(info[2 * n + 1] // HALF) % 2 for n in range(scans)]
    tile = [info[2 * scans + 2 * n] for n in range(scans)]
    live = [(n < info[4 * scans]).astype(jnp.int32) for n in range(scans)]
    zero = jnp.int32(0)
    before, after = [zero] * scans, [zero] * scans
    for two in range(scans):
        for one in range(two):
            same = (tile[one] == tile[two]) & (straddles[one] + straddles[two] == 2)
            same = same.astype(jnp.int32)
            before[two], after[one] = before[two] | same, after[one] | same
    odd = info[4 * scans + 1]
    shift = [straddles[n] * jnp.where(odd == 1, 1 - after[n], before[n]) for n in range(scans)]
    owner = [tile[n] + shift[n] for n in range(scans)]
    aside = [jnp.where(straddles[n] == 1, 1 - shift[n], 2 * odd - 1) for n in range(scans)]
    other = [lax.rem(tile[n] + aside[n] + tiles, tiles) for n in range(scans)]
    for n in range(scans):
        free = live[n] * (1 - before[n]) * (1 - after[n])
        for k in range(scans):
            if k != n:
                free = free * (1 - (owner[k] == other[n]).astype(jnp.int32))
            if k < n:
                free = free * (1 - (other[k] == other[n]).astype(jnp.int32))
        column = (jnp.where(straddles[n] == 1, 2 - 2 * shift[n], 1) + odd) & 3
        moved_column = (jnp.where(straddles[n] == 1, 2 * shift[n], 3) + odd) & 3
        note = live[n] + 2 * free + 4 * owner[n] + 64 * other[n] + 1024 * level[n]
        note = note + 4096 * column + 16384 * moved_column
        for t in range(tiles):
            notes[t, 0, n] = note
    for t in range(tiles):
        for n in range(scans, SLOTS):
            notes[t, 0, n] = 0


def assign_kernel(me, notes, packed, codes, slots, loads, homes, sems):
    tiles = codes.shape[0]
    scans = packed.shape[0]
    for t in range(tiles):
        loads[t] = 0

    @pl.loop(0, tiles)
    def _(source):
        for n in range(scans):
            note = notes[source, 0, n]
            loads[(note >> 2) & 15] += note & 1

    @pl.loop(0, tiles)
    def _(source):
        code = jnp.int32(0)
        for n in range(scans):
            note = notes[source, 0, n]
            owner, other = (note >> 2) & 15, (note >> 6) & 15
            here, there = loads[owner], loads[other]
            move = ((note >> 1) & 1) * (here > there + 1).astype(jnp.int32)
            loads[owner] = here - move
            loads[other] = loads[other] + move
            home = jnp.where(move == 1, other, owner)
            column = (note >> (12 + 2 * move)) & 3
            mine = (note & 1) * (home == me[0]).astype(jnp.int32)
            code = code + mine * (1 + 4 * ((note >> 10) & 3) + column)

            @pl.when(source == me[0])
            def _():
                homes[n] = jnp.where((note & 1) == 1, home, -1)

        codes[source] = code

    def each(act):
        for n in range(scans):

            @pl.when(homes[n] >= 0)
            def _():
                act(pltpu.make_async_copy(packed.at[n], slots.at[homes[n]], sems.at[n]))

    each(lambda copy: copy.start())
    each(lambda copy: copy.wait())


def cast_kernel(odd, obj, tile_low, half):
    side = pl.multiple_of((1 - odd[0]) * HALF, HALF)
    tile_low[...] = obj[...].astype(BF16)
    half[...] = obj[:, :, :, pl.ds(side, HALF)].astype(BF16)


def sort_kernel(info, measured, sort, packed):
    scans = measured.shape[0]
    for n in range(scans):

        @pl.when(n < info[4 * scans])
        def _():
            rows = jnp.dot(sort[1], measured[n].astype(BF16), preferred_element_type=F32)
            both = jnp.dot(rows.astype(BF16), sort[0], preferred_element_type=F32)
            packed[n] = both.astype(BF16)


def banded(taps, row, shift):
    line = jnp.broadcast_to(taps[row : row + 1, :], (SIZE, 2 * SIZE))
    return pltpu.roll(line, shift, 1, stride=1, stride_axis=0)[:, :SIZE]


STRAIGHT, TURNED = 2 * SIZE - 32, 2 * SIZE - 31


def put_table(out, real, imag, from_left):
    sign = 1.0 if from_left else -1.0
    out[:SIZE, :SIZE] = real.astype(BF16)
    out[:SIZE, SIZE:] = (-sign * imag).astype(BF16)
    out[SIZE:, :SIZE] = (sign * imag).astype(BF16)
    out[SIZE:, SIZE:] = real.astype(BF16)


def put_tables(taps, tables):
    put_table(tables.at[0], banded(taps, 0, STRAIGHT), banded(taps, 1, STRAIGHT), True)
    put_table(tables.at[1], banded(taps, 6, TURNED), banded(taps, 7, TURNED), False)


def put_adjoints(taps, tables):
    put_table(tables.at[0], banded(taps, 4, TURNED), -banded(taps, 5, TURNED), True)
    put_table(tables.at[1], banded(taps, 2, STRAIGHT), -banded(taps, 3, STRAIGHT), False)


CHUNKS = [slice(at, at + CHUNK) for at in range(0, SIZE, CHUNK)]


def in_turn(*stages):
    for step in range(MODES + len(stages) - 1):
        for place, stage in enumerate(stages):
            if 0 <= step - place < MODES:
                stage(step - place)


def rows_of(m):
    return slice(m * SIZE, (m + 1) * SIZE)


def left_stage(table, rows_in, cols_in):
    def stage(m):
        both = jnp.dot(table, rows_in[m], preferred_element_type=F32)
        cols_in[rows_of(m), :SIZE] = both[:SIZE].astype(BF16)
        cols_in[rows_of(m), SIZE:] = both[SIZE:].astype(BF16)

    return stage


def right_stage(table, cols_in, out):
    def stage(m):
        out[rows_of(m), :] = jnp.dot(cols_in[rows_of(m), :], table, preferred_element_type=F32)

    return stage


def put_rows(rows_in, m, at, real, imag):
    rows_in[m, at.start : at.stop, :] = real.astype(BF16)
    rows_in[m, SIZE + at.start : SIZE + at.stop, :] = imag.astype(BF16)


def put_halves(rows_in, m, at, first, second):
    for place, part in enumerate(first + second):
        low = place * HALF + at.start
        rows_in[m, low : low + CHUNK, :] = part.astype(BF16)


def dft_left(dft, rows_in, cols_in):
    def stage(m):
        for first in range(2):
            part = slice(first * SIZE, (first + 1) * SIZE)
            both = jnp.dot(dft[first], rows_in[m, part, :], preferred_element_type=F32)
            rows = slice(m * SIZE + first * HALF, m * SIZE + (first + 1) * HALF)
            for k in range(2):
                here = both[k * HALF : (k + 1) * HALF]
                low, high = here[:, :HALF], here[:, HALF:]
                cols_in[rows, k * HALF : (k + 1) * HALF] = (low + high).astype(BF16)
                cols_in[rows, SIZE + k * HALF : SIZE + (k + 1) * HALF] = (low - high).astype(BF16)

    return stage


def dft_right(dft, cols_in, out):
    def stage(m):
        for first in range(2):
            part = slice(first * SIZE, (first + 1) * SIZE)
            both = jnp.dot(cols_in[rows_of(m), part], dft[2 + first], preferred_element_type=F32)
            for k in range(2):
                low = k * SIZE + first * HALF
                out[rows_of(m), low : low + HALF] = both[:, k * HALF : (k + 1) * HALF]

    return stage


def inverse_left(dft, rows_in, cols_in):
    def stage(m):
        even = jnp.dot(dft[2], rows_in[m, :SIZE, :], preferred_element_type=F32)
        odd = jnp.dot(dft[3], rows_in[m, SIZE:, :], preferred_element_type=F32)
        for k in range(2):
            part = slice(k * HALF, (k + 1) * HALF)
            sums = (even[part] + odd[part]).astype(BF16)
            gaps = (even[part] - odd[part]).astype(BF16)
            for side in range(2):
                here = slice(side * HALF, (side + 1) * HALF)
                low = side * SIZE + k * HALF
                cols_in[m * SIZE : m * SIZE + HALF, low : low + HALF] = sums[:, here]
                cols_in[m * SIZE + HALF : (m + 1) * SIZE, low : low + HALF] = gaps[:, here]

    return stage


def inverse_right(dft, cols_in, out):
    def stage(m):
        even = jnp.dot(cols_in[rows_of(m), :SIZE], dft[0], preferred_element_type=F32)
        odd = jnp.dot(cols_in[rows_of(m), SIZE:], dft[1], preferred_element_type=F32)
        for k in range(2):
            part = slice(k * HALF, (k + 1) * HALF)
            out[rows_of(m), k * SIZE : k * SIZE + HALF] = even[:, part] + odd[:, part]
            out[rows_of(m), k * SIZE + HALF : (k + 1) * SIZE] = even[:, part] - odd[:, part]

    return stage


def pair(ref, m, at):
    here = slice(m * SIZE + at.start, m * SIZE + at.stop)
    return ref[here, :SIZE], ref[here, SIZE:]


def extend(odd, full, tile, half, ext):
    ext[4 * odd] = half[...]
    ext[1 + odd], ext[2 + odd] = tile[:, :, :, :HALF], tile[:, :, :, HALF:]
    ext[3 - 3 * odd], ext[4 - 3 * odd] = full[:, :, :, :HALF], full[:, :, :, HALF:]


def live_list(codes, order):
    def note(slot, found):
        live = codes[slot] > 0

        @pl.when(live)
        def _():
            order[found] = slot

        return found + live.astype(jnp.int32)

    return lax.fori_loop(0, codes.shape[0], note, jnp.int32(0))


def place_of(code):
    return (code - 1) % 4, pl.multiple_of(((code - 1) // 4) * HALF, HALF)


def pair_of(patch, s, at):
    return patch[s, at, :SIZE].astype(F32), patch[s, at, SIZE:].astype(F32)


def forward_kernel(
    odd, codes, full, tile, half, probe, taps, dft,
    moved_all, far_all, root_all, patch_all,
    ext, tables, rows_in, cols_in, moved_two, far_two, root_two, patch_two, order, sems,
):
    extend(odd[0], full, tile, half, ext)
    put_tables(taps, tables)
    found = live_list(codes, order)
    wholes = (root_all, moved_all, far_all, patch_all)
    buffers = (root_two, moved_two, far_two, patch_two)

    def copies(i):
        two = lax.rem(i, 2)
        return [
            pltpu.make_async_copy(buffers[k].at[two], wholes[k].at[order[i]], sems.at[two, k])
            for k in range(4)
        ]

    @pl.loop(0, found)
    def _(i):
        two = lax.rem(i, 2)
        root, moved, far, patch = (buffer.at[two] for buffer in buffers)

        @pl.when(i >= 2)
        def _():
            for copy in copies(i - 2):
                copy.wait()

        column, start = place_of(codes[order[i]])
        for s in range(2):
            for part in range(2):
                for side in range(2):
                    low = part * SIZE + side * HALF
                    patch[s, :, low : low + HALF] = ext[column + side, s, part, pl.ds(start, SIZE), :]

        def wave(m):
            for at in CHUNKS:
                o_re, o_im = pair_of(patch, 0, at)
                p_re, p_im = probe[m, 0, at, :].astype(F32), probe[m, 1, at, :].astype(F32)
                put_rows(rows_in, m, at, p_re * o_re - p_im * o_im, p_re * o_im + p_im * o_re)

        def exit_wave(m):
            for at in CHUNKS[: len(CHUNKS) // 2]:
                down = slice(at.start + HALF, at.stop + HALF)
                o_re, o_im = pair_of(patch, 1, at)
                q_re, q_im = pair_of(patch, 1, down)
                v_re, v_im = pair(moved, m, at)
                w_re, w_im = pair(moved, m, down)
                a_re, a_im = v_re * o_re - v_im * o_im, v_re * o_im + v_im * o_re
                b_re, b_im = w_re * q_re - w_im * q_im, w_re * q_im + w_im * q_re
                put_halves(rows_in, m, at, (a_re + b_re, a_im + b_im), (a_re - b_re, a_im - b_im))

        in_turn(
            wave,
            left_stage(tables[0], rows_in, cols_in),
            right_stage(tables[1], cols_in, moved),
            exit_wave,
            dft_left(dft, rows_in, cols_in),
            dft_right(dft, cols_in, far),
        )
        for copy in copies(i)[1:]:
            copy.start()
        for at in CHUNKS:
            power = jnp.ones((CHUNK, SIZE), F32)
            for m in range(MODES):
                f_re, f_im = pair(far, m, at)
                power = power + (f_re * f_re + f_im * f_im)
            root[at, :] = 1.0 / jnp.sqrt(power)
        copies(i)[0].start()

    for last in (2, 1):

        @pl.when(found >= last)
        def _():
            for copy in copies(found - last):
                copy.wait()


def backward_kernel(
    odd, codes, dft, taps, probe_all,
    moved_all, far_all, root_all, patch_all, slots_all,
    own_grad, full_grad, half_grad, keep, give,
    rows_in, cols_in, moved_two, far_two, root_two, patch_two, slots_two,
    factor, probe, adjoints, acc, probe_acc, order, sems, once, ends,
):
    found = live_list(codes, order)
    wholes = (far_all, slots_all, root_all, moved_all, patch_all)
    buffers = (far_two, slots_two, root_two, moved_two, patch_two)
    probe_copy = pltpu.make_async_copy(probe_all, probe, once)

    def copies(i):
        two = lax.rem(i, 2)
        return [
            pltpu.make_async_copy(wholes[k].at[order[i]], buffers[k].at[two], sems.at[two, k])
            for k in range(5)
        ]

    @pl.when(found > 0)
    def _():
        for copy in copies(0) + [probe_copy]:
            copy.start()

    put_adjoints(taps, adjoints)
    acc[...] = jnp.zeros(acc.shape, F32)
    probe_acc[...] = jnp.zeros(probe_acc.shape, F32)

    def add_piece(s, at, column, start, g_re, g_im):
        rows = pl.ds(pl.multiple_of(start + at.start, CHUNK), CHUNK)
        for part, value in ((0, g_re), (1, g_im)):
            value = value.astype(BF16).astype(F32)
            for side in range(2):
                acc[column + side, s, part, rows, :] += value[:, side * HALF : (side + 1) * HALF]

    @pl.loop(0, found)
    def _(i):
        two = lax.rem(i, 2)
        far, slot, root, moved, patch = (buffer.at[two] for buffer in buffers)

        @pl.when(i + 1 < found)
        def _():
            for copy in copies(i + 1):
                copy.start()

        column, start = place_of(codes[order[i]])
        for copy in copies(i)[:3]:
            copy.wait()

        def scaled(m):
            for at in CHUNKS[: len(CHUNKS) // 2]:
                down = slice(at.start + HALF, at.stop + HALF)
                f_re, f_im = pair(far, m, at)
                g_re, g_im = pair(far, m, down)
                top, low = factor[at, :], factor[down, :]
                put_halves(rows_in, m, at, (top * f_re, top * f_im), (low * g_re, low * g_im))

        for at in CHUNKS:
            factor[at, :] = 1.0 - slot[at, :].astype(F32) * root[at, :]
        in_turn(
            scaled,
            inverse_left(dft, rows_in, cols_in),
            inverse_right(dft, cols_in, far),
        )
        for copy in copies(i)[3:]:
            copy.wait()
        for at in CHUNKS:
            o_re, o_im = pair_of(patch, 1, at)
            g_re = jnp.zeros((CHUNK, SIZE), F32)
            g_im = jnp.zeros((CHUNK, SIZE), F32)
            for m in range(MODES):
                a_re, a_im = pair(far, m, at)
                v_re, v_im = pair(moved, m, at)
                g_re = g_re + (v_re * a_re + v_im * a_im)
                g_im = g_im + (v_re * a_im - v_im * a_re)
                put_rows(rows_in, m, at, o_re * a_re + o_im * a_im, o_re * a_im - o_im * a_re)
            add_piece(1, at, column, start, g_re, g_im)

        in_turn(
            left_stage(adjoints[0], rows_in, cols_in),
            right_stage(adjoints[1], cols_in, moved),
        )

        @pl.when(i == 0)
        def _():
            probe_copy.wait()

        for at in CHUNKS:
            o_re, o_im = pair_of(patch, 0, at)
            g_re = jnp.zeros((CHUNK, SIZE), F32)
            g_im = jnp.zeros((CHUNK, SIZE), F32)
            for m in range(MODES):
                i_re, i_im = pair(moved, m, at)
                p_re, p_im = probe[m, 0, at, :].astype(F32), probe[m, 1, at, :].astype(F32)
                g_re = g_re + (p_re * i_re + p_im * i_im)
                g_im = g_im + (p_re * i_im - p_im * i_re)
                probe_acc[m, 0, at, :] += o_re * i_re + o_im * i_im
                probe_acc[m, 1, at, :] += o_re * i_im - o_im * i_re
            add_piece(0, at, column, start, g_re, g_im)

    leave = [
        pltpu.make_async_copy(
            acc.at[1 + side + odd[0]],
            own_grad.at[:, :, :, pl.ds(side * HALF, HALF)],
            ends.at[side],
        )
        for side in range(2)
    ]
    for copy in leave:
        copy.start()
    half_grad[...] = acc[4 * odd[0]].astype(BF16)
    full_grad[:, :, :, :HALF] = acc[3 - 3 * odd[0]].astype(BF16)
    full_grad[:, :, :, HALF:] = acc[4 - 3 * odd[0]].astype(BF16)
    modes = MODES // 2
    keep[...] = probe_acc[pl.ds(modes * odd[0], modes)].astype(BF16)
    give[...] = probe_acc[pl.ds(modes * (1 - odd[0]), modes)].astype(BF16)
    for copy in leave:
        copy.wait()


def whole(count):
    return [pl.BlockSpec(memory_space=pltpu.VMEM) for _ in range(count)]


def scalars(count):
    return [pl.BlockSpec(memory_space=pltpu.SMEM) for _ in range(count)]


def body(object_slices, probe, measured, tap_row, tap_col, scan_corner, correlation, scan_count):
    cols = lax.axis_size("col")
    rows = lax.axis_size("row")
    band = object_slices.shape[2]
    part_shape = (2, 2, band, HALF)
    limit = pltpu.CompilerParams(vmem_limit_bytes=56 * 1024 * 1024)

    tile_shape = (2, 2, band, SIZE)
    scans = measured.shape[0]
    odd = (lax.axis_index("row") % 2).reshape(1)
    def anywhere(count):
        return [pl.BlockSpec(memory_space=pl.ANY) for _ in range(count)]

    def ring(step):
        pairs = []
        for r in range(rows):
            way = step if r % 2 == 0 else -step
            pairs += [(r * cols + c, r * cols + (c + way) % cols) for c in range(cols)]
        return pairs

    both = ("row", "col")
    tile_low, half = pl.pallas_call(
        cast_kernel,
        out_shape=[
            jax.ShapeDtypeStruct(tile_shape, BF16),
            jax.ShapeDtypeStruct(part_shape, BF16),
        ],
        in_specs=scalars(1) + whole(1),
        out_specs=whole(2),
        compiler_params=limit,
    )(odd, object_slices)
    full = lax.ppermute(tile_low, both, ring(-1))
    half = lax.ppermute(half, both, ring(1))

    info = [scan_corner.reshape(-1), correlation.reshape(-1), scan_count.reshape(-1), odd]
    info = jnp.concatenate(info)
    notes = pl.pallas_call(
        describe_kernel,
        out_shape=jax.ShapeDtypeStruct((cols, 1, SLOTS), jnp.int32),
        in_specs=scalars(1),
        out_specs=pl.BlockSpec(memory_space=pltpu.SMEM),
        compiler_params=limit,
    )(info)
    row_notes = lax.all_to_all(notes, "col", split_axis=0, concat_axis=0, tiled=True)
    packed = pl.pallas_call(
        sort_kernel,
        out_shape=jax.ShapeDtypeStruct((scans, SIZE, SIZE), BF16),
        in_specs=scalars(1) + whole(2),
        out_specs=pl.BlockSpec(memory_space=pltpu.VMEM),
        compiler_params=limit,
    )(info, measured, sorter())
    codes, slots = pl.pallas_call(
        assign_kernel,
        out_shape=[
            jax.ShapeDtypeStruct((cols,), jnp.int32),
            jax.ShapeDtypeStruct((cols, SIZE, SIZE), BF16),
        ],
        in_specs=scalars(2) + whole(1),
        out_specs=scalars(1) + anywhere(1),
        scratch_shapes=[
            pltpu.SMEM((cols,), jnp.int32),
            pltpu.SMEM((scans,), jnp.int32),
            pltpu.SemaphoreType.DMA((scans,)),
        ],
        compiler_params=limit,
    )(lax.axis_index("col").reshape(1), row_notes, packed)
    arrived = lax.all_to_all(slots, "col", split_axis=0, concat_axis=0, tiled=True)

    taps = jnp.concatenate([tap_row, tap_col], axis=0)
    taps = jnp.concatenate([taps, taps[:, ::-1]], axis=0)
    taps = jnp.pad(taps, ((0, 0), (0, 2 * SIZE - taps.shape[1])))
    dft = dft_tables()

    field_shape = (MODES * SIZE, 2 * SIZE)
    patch_shape = (2, SIZE, 2 * SIZE)
    pair_shape = (2, 2 * SIZE, 2 * SIZE)
    work = [
        pltpu.VMEM((MODES, 2 * SIZE, SIZE), BF16),
        pltpu.VMEM(field_shape, BF16),
        pltpu.VMEM((2,) + field_shape, F32),
        pltpu.VMEM((2,) + field_shape, F32),
        pltpu.VMEM((2, SIZE, SIZE), F32),
        pltpu.VMEM((2,) + patch_shape, BF16),
    ]
    order = pltpu.SMEM((cols,), jnp.int32)
    moved_all, far_all, root_all, patch_all = pl.pallas_call(
        forward_kernel,
        out_shape=[
            jax.ShapeDtypeStruct((cols,) + field_shape, F32),
            jax.ShapeDtypeStruct((cols,) + field_shape, F32),
            jax.ShapeDtypeStruct((cols, SIZE, SIZE), F32),
            jax.ShapeDtypeStruct((cols,) + patch_shape, BF16),
        ],
        in_specs=scalars(2) + whole(6),
        out_specs=anywhere(4),
        scratch_shapes=[pltpu.VMEM((5,) + part_shape, BF16), pltpu.VMEM(pair_shape, BF16)]
        + work
        + [order, pltpu.SemaphoreType.DMA((2, 4))],
        cost_estimate=pl.CostEstimate(flops=40 * 10**9, bytes_accessed=10**7, transcendentals=0),
        compiler_params=limit,
    )(odd, codes, full, tile_low, half, probe, taps, dft)
    half_probe = (MODES // 2,) + probe.shape[1:]
    own_grad, full_grad, half_grad, keep, give = pl.pallas_call(
        backward_kernel,
        out_shape=[
            jax.ShapeDtypeStruct(tile_shape, F32),
            jax.ShapeDtypeStruct(tile_shape, BF16),
            jax.ShapeDtypeStruct(part_shape, BF16),
            jax.ShapeDtypeStruct(half_probe, BF16),
            jax.ShapeDtypeStruct(half_probe, BF16),
        ],
        in_specs=scalars(2) + whole(2) + anywhere(6),
        out_specs=anywhere(1) + whole(4),
        scratch_shapes=work
        + [
            pltpu.VMEM((2, SIZE, SIZE), BF16),
            pltpu.VMEM((SIZE, SIZE), F32),
            pltpu.VMEM(probe.shape, BF16),
            pltpu.VMEM(pair_shape, BF16),
            pltpu.VMEM((5,) + part_shape, F32),
            pltpu.VMEM(probe.shape, F32),
            order,
            pltpu.SemaphoreType.DMA((2, 5)),
            pltpu.SemaphoreType.DMA,
            pltpu.SemaphoreType.DMA((2,)),
        ],
        compiler_params=limit,
    )(
        odd, codes, dft, taps, probe,
        moved_all, far_all, root_all, patch_all, arrived,
    )

    full_grad = lax.ppermute(full_grad, both, ring(1))
    half_grad = lax.ppermute(half_grad, both, ring(-1))
    share = MODES * SIZE // cols
    partner = [(r * cols + c, (r ^ 1) * cols + c) for r in range(rows) for c in range(cols)]

    def swap(blocks, axis):
        return lax.all_to_all(blocks, axis, split_axis=0, concat_axis=0, tiled=True)

    given = lax.ppermute(give, both, partner)
    mine = (keep.astype(F32) + given.astype(F32)).astype(BF16)
    mine = swap(mine.reshape(cols, share, SIZE), "col")
    mine = jnp.sum(mine.astype(F32), axis=0).astype(BF16)
    mine = swap(jnp.broadcast_to(mine[None], (rows, share, SIZE)), "row")
    same = (jnp.arange(rows) % 2 == odd[0]).astype(F32)
    scale = 1.0 / math.sqrt(scans * cols * rows)
    mine = (jnp.sum(mine.astype(F32) * same[:, None, None], axis=0) * scale).astype(BF16)
    mine, full_grad, half_grad = lax.optimization_barrier((mine, full_grad, half_grad))
    mine = swap(jnp.broadcast_to(mine[None], (cols, share, SIZE)), "col").reshape(half_probe)
    given = lax.ppermute(mine, both, partner)
    even = odd[0] == 0
    probe_grad = [jnp.where(even, mine, given), jnp.where(even, given, mine)]
    probe_grad = jnp.concatenate(probe_grad, axis=0).astype(F32)
    half_grad = half_grad.astype(F32)
    nothing = jnp.zeros_like(half_grad)
    odd = odd[0] == 1
    halo = [jnp.where(odd, half_grad, nothing), jnp.where(odd, nothing, half_grad)]
    return own_grad + full_grad.astype(F32) + jnp.concatenate(halo, axis=-1), probe_grad


def solution(mesh):
    in_specs = (
        P(None, None, "row", "col"),
        P(),
        P(("row", "col"), None, None),
        P(),
        P(),
        P(("row", "col"), None),
        P(("row", "col"), None),
        P("row", "col"),
    )
    out_specs = (P(None, None, "row", "col"), P())
    return jax.shard_map(body, mesh=mesh, in_specs=in_specs, out_specs=out_specs, check_vma=False)
```

```python
import math

import jax
import jax.numpy as jnp
import numpy as np
from jax import lax
from jax.experimental import pallas as pl
from jax.experimental.pallas import tpu as pltpu
from jax.sharding import PartitionSpec as P

SIZE = 256
HALF = 128
MODES = 4
CHUNK = 16
SLOTS = 8
BF16 = jnp.bfloat16
F32 = jnp.float32


def dft_tables():
    index = np.arange(SIZE)
    phase = 2.0 * np.pi * ((index[:, None] * index[None, :]) % SIZE) / SIZE
    real = np.cos(phase) / math.sqrt(SIZE)
    imag = -np.sin(phase) / math.sqrt(SIZE)
    halves = []
    for first in range(2):
        re, im = real[first::2, :HALF], imag[first::2, :HALF]
        halves.append(np.block([[re, -im], [im, re]]))
    both = np.stack(halves + [half.T for half in halves])
    return jnp.asarray(both, F32).astype(BF16)


def sorter():
    index = np.arange(SIZE)
    place = index // 2 + HALF * (index % 2)
    sort = place[:, None] == index[None, :]
    return jnp.asarray(np.stack([sort, sort.T]), BF16)


def describe_kernel(info, notes):
    tiles = notes.shape[0]
    scans = (info.shape[0] - 2) // 4
    level = [(info[2 * n] // HALF) % 4 for n in range(scans)]
    straddles = [(info[2 * n + 1] // HALF) % 2 for n in range(scans)]
    tile = [info[2 * scans + 2 * n] for n in range(scans)]
    live = [(n < info[4 * scans]).astype(jnp.int32) for n in range(scans)]
    zero = jnp.int32(0)
    before, after = [zero] * scans, [zero] * scans
    for two in range(scans):
        for one in range(two):
            same = (tile[one] == tile[two]) & (straddles[one] + straddles[two] == 2)
            same = same.astype(jnp.int32)
            before[two], after[one] = before[two] | same, after[one] | same
    odd = info[4 * scans + 1]
    shift = [straddles[n] * jnp.where(odd == 1, 1 - after[n], before[n]) for n in range(scans)]
    owner = [tile[n] + shift[n] for n in range(scans)]
    aside = [jnp.where(straddles[n] == 1, 1 - shift[n], 2 * odd - 1) for n in range(scans)]
    other = [lax.rem(tile[n] + aside[n] + tiles, tiles) for n in range(scans)]
    for n in range(scans):
        free = live[n] * (1 - before[n]) * (1 - after[n])
        for k in range(scans):
            if k != n:
                free = free * (1 - (owner[k] == other[n]).astype(jnp.int32))
            if k < n:
                free = free * (1 - (other[k] == other[n]).astype(jnp.int32))
        column = (jnp.where(straddles[n] == 1, 2 - 2 * shift[n], 1) + odd) & 3
        moved_column = (jnp.where(straddles[n] == 1, 2 * shift[n], 3) + odd) & 3
        note = live[n] + 2 * free + 4 * owner[n] + 64 * other[n] + 1024 * level[n]
        note = note + 4096 * column + 16384 * moved_column
        for t in range(tiles):
            notes[t, 0, n] = note
    for t in range(tiles):
        for n in range(scans, SLOTS):
            notes[t, 0, n] = 0


def assign_kernel(me, notes, packed, codes, slots, loads, homes, sems):
    tiles = codes.shape[0]
    scans = packed.shape[0]
    for t in range(tiles):
        loads[t] = 0

    @pl.loop(0, tiles)
    def _(source):
        for n in range(scans):
            note = notes[source, 0, n]
            loads[(note >> 2) & 15] += note & 1

    @pl.loop(0, tiles)
    def _(source):
        code = jnp.int32(0)
        for n in range(scans):
            note = notes[source, 0, n]
            owner, other = (note >> 2) & 15, (note >> 6) & 15
            here, there = loads[owner], loads[other]
            move = ((note >> 1) & 1) * (here > there + 1).astype(jnp.int32)
            loads[owner] = here - move
            loads[other] = loads[other] + move
            home = jnp.where(move == 1, other, owner)
            column = (note >> (12 + 2 * move)) & 3
            mine = (note & 1) * (home == me[0]).astype(jnp.int32)
            code = code + mine * (1 + 4 * ((note >> 10) & 3) + column)

            @pl.when(source == me[0])
            def _():
                homes[n] = jnp.where((note & 1) == 1, home, -1)

        codes[source] = code

    def each(act):
        for n in range(scans):

            @pl.when(homes[n] >= 0)
            def _():
                act(pltpu.make_async_copy(packed.at[n], slots.at[homes[n]], sems.at[n]))

    each(lambda copy: copy.start())
    each(lambda copy: copy.wait())


def cast_kernel(odd, obj, tile_low, half):
    side = pl.multiple_of((1 - odd[0]) * HALF, HALF)
    tile_low[...] = obj[...].astype(BF16)
    half[...] = obj[:, :, :, pl.ds(side, HALF)].astype(BF16)


def sort_kernel(info, measured, sort, packed):
    scans = measured.shape[0]
    for n in range(scans):

        @pl.when(n < info[4 * scans])
        def _():
            rows = jnp.dot(sort[1], measured[n].astype(BF16), preferred_element_type=F32)
            both = jnp.dot(rows.astype(BF16), sort[0], preferred_element_type=F32)
            packed[n] = both.astype(BF16)


def banded(taps, row, shift):
    line = jnp.broadcast_to(taps[row : row + 1, :], (SIZE, 2 * SIZE))
    return pltpu.roll(line, shift, 1, stride=1, stride_axis=0)[:, :SIZE]


STRAIGHT, TURNED = 2 * SIZE - 32, 2 * SIZE - 31


def put_table(out, real, imag, from_left):
    sign = 1.0 if from_left else -1.0
    out[:SIZE, :SIZE] = real.astype(BF16)
    out[:SIZE, SIZE:] = (-sign * imag).astype(BF16)
    out[SIZE:, :SIZE] = (sign * imag).astype(BF16)
    out[SIZE:, SIZE:] = real.astype(BF16)


def put_tables(taps, tables):
    put_table(tables.at[0], banded(taps, 0, STRAIGHT), banded(taps, 1, STRAIGHT), True)
    put_table(tables.at[1], banded(taps, 6, TURNED), banded(taps, 7, TURNED), False)


def put_adjoints(taps, tables):
    put_table(tables.at[0], banded(taps, 4, TURNED), -banded(taps, 5, TURNED), True)
    put_table(tables.at[1], banded(taps, 2, STRAIGHT), -banded(taps, 3, STRAIGHT), False)


CHUNKS = [slice(at, at + CHUNK) for at in range(0, SIZE, CHUNK)]


def in_turn(*stages):
    for step in range(MODES + len(stages) - 1):
        for place, stage in enumerate(stages):
            if 0 <= step - place < MODES:
                stage(step - place)


def rows_of(m):
    return slice(m * SIZE, (m + 1) * SIZE)


def left_stage(table, rows_in, cols_in):
    def stage(m):
        both = jnp.dot(table, rows_in[m], preferred_element_type=F32)
        cols_in[rows_of(m), :SIZE] = both[:SIZE].astype(BF16)
        cols_in[rows_of(m), SIZE:] = both[SIZE:].astype(BF16)

    return stage


def right_stage(table, cols_in, out):
    def stage(m):
        out[rows_of(m), :] = jnp.dot(cols_in[rows_of(m), :], table, preferred_element_type=F32)

    return stage


def put_rows(rows_in, m, at, real, imag):
    rows_in[m, at.start : at.stop, :] = real.astype(BF16)
    rows_in[m, SIZE + at.start : SIZE + at.stop, :] = imag.astype(BF16)


def put_halves(rows_in, m, at, first, second):
    for place, part in enumerate(first + second):
        low = place * HALF + at.start
        rows_in[m, low : low + CHUNK, :] = part.astype(BF16)


def dft_left(dft, rows_in, cols_in):
    def stage(m):
        for first in range(2):
            part = slice(first * SIZE, (first + 1) * SIZE)
            both = jnp.dot(dft[first], rows_in[m, part, :], preferred_element_type=F32)
            rows = slice(m * SIZE + first * HALF, m * SIZE + (first + 1) * HALF)
            for k in range(2):
                here = both[k * HALF : (k + 1) * HALF]
                low, high = here[:, :HALF], here[:, HALF:]
                cols_in[rows, k * HALF : (k + 1) * HALF] = (low + high).astype(BF16)
                cols_in[rows, SIZE + k * HALF : SIZE + (k + 1) * HALF] = (low - high).astype(BF16)

    return stage


def dft_right(dft, cols_in, out):
    def stage(m):
        for first in range(2):
            part = slice(first * SIZE, (first + 1) * SIZE)
            both = jnp.dot(cols_in[rows_of(m), part], dft[2 + first], preferred_element_type=F32)
            for k in range(2):
                low = k * SIZE + first * HALF
                out[rows_of(m), low : low + HALF] = both[:, k * HALF : (k + 1) * HALF]

    return stage


def inverse_left(dft, rows_in, cols_in):
    def stage(m):
        even = jnp.dot(dft[2], rows_in[m, :SIZE, :], preferred_element_type=F32)
        odd = jnp.dot(dft[3], rows_in[m, SIZE:, :], preferred_element_type=F32)
        for k in range(2):
            part = slice(k * HALF, (k + 1) * HALF)
            sums = (even[part] + odd[part]).astype(BF16)
            gaps = (even[part] - odd[part]).astype(BF16)
            for side in range(2):
                here = slice(side * HALF, (side + 1) * HALF)
                low = side * SIZE + k * HALF
                cols_in[m * SIZE : m * SIZE + HALF, low : low + HALF] = sums[:, here]
                cols_in[m * SIZE + HALF : (m + 1) * SIZE, low : low + HALF] = gaps[:, here]

    return stage


def inverse_right(dft, cols_in, out):
    def stage(m):
        even = jnp.dot(cols_in[rows_of(m), :SIZE], dft[0], preferred_element_type=F32)
        odd = jnp.dot(cols_in[rows_of(m), SIZE:], dft[1], preferred_element_type=F32)
        for k in range(2):
            part = slice(k * HALF, (k + 1) * HALF)
            out[rows_of(m), k * SIZE : k * SIZE + HALF] = even[:, part] + odd[:, part]
            out[rows_of(m), k * SIZE + HALF : (k + 1) * SIZE] = even[:, part] - odd[:, part]

    return stage


def pair(ref, m, at):
    here = slice(m * SIZE + at.start, m * SIZE + at.stop)
    return ref[here, :SIZE], ref[here, SIZE:]


def extend(odd, full, tile, half, ext):
    ext[4 * odd] = half[...]
    ext[1 + odd], ext[2 + odd] = tile[:, :, :, :HALF], tile[:, :, :, HALF:]
    ext[3 - 3 * odd], ext[4 - 3 * odd] = full[:, :, :, :HALF], full[:, :, :, HALF:]


def live_list(codes, order):
    def note(slot, found):
        live = codes[slot] > 0

        @pl.when(live)
        def _():
            order[found] = slot

        return found + live.astype(jnp.int32)

    return lax.fori_loop(0, codes.shape[0], note, jnp.int32(0))


def place_of(code):
    return (code - 1) % 4, pl.multiple_of(((code - 1) // 4) * HALF, HALF)


def pair_of(patch, s, at):
    return patch[s, at, :SIZE].astype(F32), patch[s, at, SIZE:].astype(F32)


def forward_kernel(
    odd, codes, full, tile, half, probe, taps, dft,
    moved_all, far_all, root_all, patch_all,
    ext, tables, rows_in, cols_in, moved_two, far_two, root_two, patch_two, order, sems,
):
    extend(odd[0], full, tile, half, ext)
    put_tables(taps, tables)
    found = live_list(codes, order)
    wholes = (root_all, moved_all, far_all, patch_all)
    buffers = (root_two, moved_two, far_two, patch_two)

    def copies(i):
        two = lax.rem(i, 2)
        return [
            pltpu.make_async_copy(buffers[k].at[two], wholes[k].at[order[i]], sems.at[two, k])
            for k in range(4)
        ]

    @pl.loop(0, found)
    def _(i):
        two = lax.rem(i, 2)
        root, moved, far, patch = (buffer.at[two] for buffer in buffers)

        @pl.when(i >= 2)
        def _():
            for copy in copies(i - 2):
                copy.wait()

        column, start = place_of(codes[order[i]])
        for s in range(2):
            for part in range(2):
                for side in range(2):
                    low = part * SIZE + side * HALF
                    patch[s, :, low : low + HALF] = ext[column + side, s, part, pl.ds(start, SIZE), :]

        def wave(m):
            for at in CHUNKS:
                o_re, o_im = pair_of(patch, 0, at)
                p_re, p_im = probe[m, 0, at, :].astype(F32), probe[m, 1, at, :].astype(F32)
                put_rows(rows_in, m, at, p_re * o_re - p_im * o_im, p_re * o_im + p_im * o_re)

        def exit_wave(m):
            for at in CHUNKS[: len(CHUNKS) // 2]:
                down = slice(at.start + HALF, at.stop + HALF)
                o_re, o_im = pair_of(patch, 1, at)
                q_re, q_im = pair_of(patch, 1, down)
                v_re, v_im = pair(moved, m, at)
                w_re, w_im = pair(moved, m, down)
                a_re, a_im = v_re * o_re - v_im * o_im, v_re * o_im + v_im * o_re
                b_re, b_im = w_re * q_re - w_im * q_im, w_re * q_im + w_im * q_re
                put_halves(rows_in, m, at, (a_re + b_re, a_im + b_im), (a_re - b_re, a_im - b_im))

        in_turn(
            wave,
            left_stage(tables[0], rows_in, cols_in),
            right_stage(tables[1], cols_in, moved),
            exit_wave,
            dft_left(dft, rows_in, cols_in),
            dft_right(dft, cols_in, far),
        )
        for copy in copies(i)[1:]:
            copy.start()
        for at in CHUNKS:
            power = jnp.ones((CHUNK, SIZE), F32)
            for m in range(MODES):
                f_re, f_im = pair(far, m, at)
                power = power + (f_re * f_re + f_im * f_im)
            root[at, :] = 1.0 / jnp.sqrt(power)
        copies(i)[0].start()

    for last in (2, 1):

        @pl.when(found >= last)
        def _():
            for copy in copies(found - last):
                copy.wait()


def backward_kernel(
    odd, codes, dft, taps, probe_all,
    moved_all, far_all, root_all, patch_all, slots_all,
    own_grad, full_grad, half_grad, keep, give,
    rows_in, cols_in, moved_two, far_two, root_two, patch_two, slots_two,
    factor, probe, adjoints, acc, probe_acc, order, sems, once, ends,
):
    found = live_list(codes, order)
    wholes = (far_all, slots_all, root_all, moved_all, patch_all)
    buffers = (far_two, slots_two, root_two, moved_two, patch_two)
    probe_copy = pltpu.make_async_copy(probe_all, probe, once)

    def copies(i):
        two = lax.rem(i, 2)
        return [
            pltpu.make_async_copy(wholes[k].at[order[i]], buffers[k].at[two], sems.at[two, k])
            for k in range(5)
        ]

    @pl.when(found > 0)
    def _():
        for copy in copies(0) + [probe_copy]:
            copy.start()

    put_adjoints(taps, adjoints)
    acc[...] = jnp.zeros(acc.shape, F32)
    probe_acc[...] = jnp.zeros(probe_acc.shape, F32)

    def add_piece(s, at, column, start, g_re, g_im):
        rows = pl.ds(pl.multiple_of(start + at.start, CHUNK), CHUNK)
        for part, value in ((0, g_re), (1, g_im)):
            value = value.astype(BF16).astype(F32)
            for side in range(2):
                acc[column + side, s, part, rows, :] += value[:, side * HALF : (side + 1) * HALF]

    @pl.loop(0, found)
    def _(i):
        two = lax.rem(i, 2)
        far, slot, root, moved, patch = (buffer.at[two] for buffer in buffers)

        @pl.when(i + 1 < found)
        def _():
            for copy in copies(i + 1):
                copy.start()

        column, start = place_of(codes[order[i]])
        for copy in copies(i)[:3]:
            copy.wait()

        def scaled(m):
            for at in CHUNKS[: len(CHUNKS) // 2]:
                down = slice(at.start + HALF, at.stop + HALF)
                f_re, f_im = pair(far, m, at)
                g_re, g_im = pair(far, m, down)
                top, low = factor[at, :], factor[down, :]
                put_halves(rows_in, m, at, (top * f_re, top * f_im), (low * g_re, low * g_im))

        for at in CHUNKS:
            factor[at, :] = 1.0 - slot[at, :].astype(F32) * root[at, :]
        in_turn(
            scaled,
            inverse_left(dft, rows_in, cols_in),
            inverse_right(dft, cols_in, far),
        )
        for copy in copies(i)[3:]:
            copy.wait()
        for at in CHUNKS:
            o_re, o_im = pair_of(patch, 1, at)
            g_re = jnp.zeros((CHUNK, SIZE), F32)
            g_im = jnp.zeros((CHUNK, SIZE), F32)
            for m in range(MODES):
                a_re, a_im = pair(far, m, at)
                v_re, v_im = pair(moved, m, at)
                g_re = g_re + (v_re * a_re + v_im * a_im)
                g_im = g_im + (v_re * a_im - v_im * a_re)
                put_rows(rows_in, m, at, o_re * a_re + o_im * a_im, o_re * a_im - o_im * a_re)
            add_piece(1, at, column, start, g_re, g_im)

        in_turn(
            left_stage(adjoints[0], rows_in, cols_in),
            right_stage(adjoints[1], cols_in, moved),
        )

        @pl.when(i == 0)
        def _():
            probe_copy.wait()

        for at in CHUNKS:
            o_re, o_im = pair_of(patch, 0, at)
            g_re = jnp.zeros((CHUNK, SIZE), F32)
            g_im = jnp.zeros((CHUNK, SIZE), F32)
            for m in range(MODES):
                i_re, i_im = pair(moved, m, at)
                p_re, p_im = probe[m, 0, at, :].astype(F32), probe[m, 1, at, :].astype(F32)
                g_re = g_re + (p_re * i_re + p_im * i_im)
                g_im = g_im + (p_re * i_im - p_im * i_re)
                probe_acc[m, 0, at, :] += o_re * i_re + o_im * i_im
                probe_acc[m, 1, at, :] += o_re * i_im - o_im * i_re
            add_piece(0, at, column, start, g_re, g_im)

    leave = [
        pltpu.make_async_copy(
            acc.at[1 + side + odd[0]],
            own_grad.at[:, :, :, pl.ds(side * HALF, HALF)],
            ends.at[side],
        )
        for side in range(2)
    ]
    for copy in leave:
        copy.start()
    half_grad[...] = acc[4 * odd[0]].astype(BF16)
    full_grad[:, :, :, :HALF] = acc[3 - 3 * odd[0]].astype(BF16)
    full_grad[:, :, :, HALF:] = acc[4 - 3 * odd[0]].astype(BF16)
    modes = MODES // 2
    keep[...] = probe_acc[pl.ds(modes * odd[0], modes)].astype(BF16)
    give[...] = probe_acc[pl.ds(modes * (1 - odd[0]), modes)].astype(BF16)
    for copy in leave:
        copy.wait()


def whole(count):
    return [pl.BlockSpec(memory_space=pltpu.VMEM) for _ in range(count)]


def scalars(count):
    return [pl.BlockSpec(memory_space=pltpu.SMEM) for _ in range(count)]


def body(object_slices, probe, measured, tap_row, tap_col, scan_corner, correlation, scan_count):
    cols = lax.axis_size("col")
    rows = lax.axis_size("row")
    band = object_slices.shape[2]
    part_shape = (2, 2, band, HALF)
    limit = pltpu.CompilerParams(vmem_limit_bytes=56 * 1024 * 1024)

    tile_shape = (2, 2, band, SIZE)
    scans = measured.shape[0]
    odd = (lax.axis_index("row") % 2).reshape(1)
    def anywhere(count):
        return [pl.BlockSpec(memory_space=pl.ANY) for _ in range(count)]

    def ring(step):
        pairs = []
        for r in range(rows):
            way = step if r % 2 == 0 else -step
            pairs += [(r * cols + c, r * cols + (c + way) % cols) for c in range(cols)]
        return pairs

    both = ("row", "col")
    tile_low, half = pl.pallas_call(
        cast_kernel,
        out_shape=[
            jax.ShapeDtypeStruct(tile_shape, BF16),
            jax.ShapeDtypeStruct(part_shape, BF16),
        ],
        in_specs=scalars(1) + whole(1),
        out_specs=whole(2),
        compiler_params=limit,
    )(odd, object_slices)
    full = lax.ppermute(tile_low, both, ring(-1))
    half = lax.ppermute(half, both, ring(1))

    info = [scan_corner.reshape(-1), correlation.reshape(-1), scan_count.reshape(-1), odd]
    info = jnp.concatenate(info)
    notes = pl.pallas_call(
        describe_kernel,
        out_shape=jax.ShapeDtypeStruct((cols, 1, SLOTS), jnp.int32),
        in_specs=scalars(1),
        out_specs=pl.BlockSpec(memory_space=pltpu.SMEM),
        compiler_params=limit,
    )(info)
    row_notes = lax.all_to_all(notes, "col", split_axis=0, concat_axis=0, tiled=True)
    packed = pl.pallas_call(
        sort_kernel,
        out_shape=jax.ShapeDtypeStruct((scans, SIZE, SIZE), BF16),
        in_specs=scalars(1) + whole(2),
        out_specs=pl.BlockSpec(memory_space=pltpu.VMEM),
        compiler_params=limit,
    )(info, measured, sorter())
    codes, slots = pl.pallas_call(
        assign_kernel,
        out_shape=[
            jax.ShapeDtypeStruct((cols,), jnp.int32),
            jax.ShapeDtypeStruct((cols, SIZE, SIZE), BF16),
        ],
        in_specs=scalars(2) + whole(1),
        out_specs=scalars(1) + anywhere(1),
        scratch_shapes=[
            pltpu.SMEM((cols,), jnp.int32),
            pltpu.SMEM((scans,), jnp.int32),
            pltpu.SemaphoreType.DMA((scans,)),
        ],
        compiler_params=limit,
    )(lax.axis_index("col").reshape(1), row_notes, packed)
    arrived = lax.all_to_all(slots, "col", split_axis=0, concat_axis=0, tiled=True)

    taps = jnp.concatenate([tap_row, tap_col], axis=0)
    taps = jnp.concatenate([taps, taps[:, ::-1]], axis=0)
    taps = jnp.pad(taps, ((0, 0), (0, 2 * SIZE - taps.shape[1])))
    dft = dft_tables()

    field_shape = (MODES * SIZE, 2 * SIZE)
    patch_shape = (2, SIZE, 2 * SIZE)
    pair_shape = (2, 2 * SIZE, 2 * SIZE)
    work = [
        pltpu.VMEM((MODES, 2 * SIZE, SIZE), BF16),
        pltpu.VMEM(field_shape, BF16),
        pltpu.VMEM((2,) + field_shape, F32),
        pltpu.VMEM((2,) + field_shape, F32),
        pltpu.VMEM((2, SIZE, SIZE), F32),
        pltpu.VMEM((2,) + patch_shape, BF16),
    ]
    order = pltpu.SMEM((cols,), jnp.int32)
    moved_all, far_all, root_all, patch_all = pl.pallas_call(
        forward_kernel,
        out_shape=[
            jax.ShapeDtypeStruct((cols,) + field_shape, F32),
            jax.ShapeDtypeStruct((cols,) + field_shape, F32),
            jax.ShapeDtypeStruct((cols, SIZE, SIZE), F32),
            jax.ShapeDtypeStruct((cols,) + patch_shape, BF16),
        ],
        in_specs=scalars(2) + whole(6),
        out_specs=anywhere(4),
        scratch_shapes=[pltpu.VMEM((5,) + part_shape, BF16), pltpu.VMEM(pair_shape, BF16)]
        + work
        + [order, pltpu.SemaphoreType.DMA((2, 4))],
        cost_estimate=pl.CostEstimate(flops=40 * 10**9, bytes_accessed=10**7, transcendentals=0),
        compiler_params=limit,
    )(odd, codes, full, tile_low, half, probe, taps, dft)
    half_probe = (MODES // 2,) + probe.shape[1:]
    own_grad, full_grad, half_grad, keep, give = pl.pallas_call(
        backward_kernel,
        out_shape=[
            jax.ShapeDtypeStruct(tile_shape, F32),
            jax.ShapeDtypeStruct(tile_shape, BF16),
            jax.ShapeDtypeStruct(part_shape, BF16),
            jax.ShapeDtypeStruct(half_probe, BF16),
            jax.ShapeDtypeStruct(half_probe, BF16),
        ],
        in_specs=scalars(2) + whole(2) + anywhere(6),
        out_specs=anywhere(1) + whole(4),
        scratch_shapes=work
        + [
            pltpu.VMEM((2, SIZE, SIZE), BF16),
            pltpu.VMEM((SIZE, SIZE), F32),
            pltpu.VMEM(probe.shape, BF16),
            pltpu.VMEM(pair_shape, BF16),
            pltpu.VMEM((5,) + part_shape, F32),
            pltpu.VMEM(probe.shape, F32),
            order,
            pltpu.SemaphoreType.DMA((2, 5)),
            pltpu.SemaphoreType.DMA,
            pltpu.SemaphoreType.DMA((2,)),
        ],
        compiler_params=limit,
    )(
        odd, codes, dft, taps, probe,
        moved_all, far_all, root_all, patch_all, arrived,
    )

    share = MODES * SIZE // cols
    partner = [(r * cols + c, (r ^ 1) * cols + c) for r in range(rows) for c in range(cols)]

    def swap(blocks, axis):
        return lax.all_to_all(blocks, axis, split_axis=0, concat_axis=0, tiled=True)

    given = lax.ppermute(give, both, partner)
    mine = (keep.astype(F32) + given.astype(F32)).astype(BF16)
    mine = swap(mine.reshape(cols, share, SIZE), "col")
    mine = jnp.sum(mine.astype(F32), axis=0).astype(BF16)
    mine, full_grad, half_grad = lax.optimization_barrier((mine, full_grad, half_grad))
    full_grad = lax.ppermute(full_grad, both, ring(1))
    half_grad = lax.ppermute(half_grad, both, ring(-1))
    mine = swap(jnp.broadcast_to(mine[None], (rows, share, SIZE)), "row")
    same = (jnp.arange(rows) % 2 == odd[0]).astype(F32)
    scale = 1.0 / math.sqrt(scans * cols * rows)
    mine = (jnp.sum(mine.astype(F32) * same[:, None, None], axis=0) * scale).astype(BF16)
    mine, full_grad, half_grad = lax.optimization_barrier((mine, full_grad, half_grad))
    mine = swap(jnp.broadcast_to(mine[None], (cols, share, SIZE)), "col").reshape(half_probe)
    given = lax.ppermute(mine, both, partner)
    even = odd[0] == 0
    probe_grad = [jnp.where(even, mine, given), jnp.where(even, given, mine)]
    probe_grad = jnp.concatenate(probe_grad, axis=0).astype(F32)
    half_grad = half_grad.astype(F32)
    nothing = jnp.zeros_like(half_grad)
    odd = odd[0] == 1
    halo = [jnp.where(odd, half_grad, nothing), jnp.where(odd, nothing, half_grad)]
    return own_grad + full_grad.astype(F32) + jnp.concatenate(halo, axis=-1), probe_grad


def solution(mesh):
    in_specs = (
        P(None, None, "row", "col"),
        P(),
        P(("row", "col"), None, None),
        P(),
        P(),
        P(("row", "col"), None),
        P(("row", "col"), None),
        P("row", "col"),
    )
    out_specs = (P(None, None, "row", "col"), P())
    return jax.shard_map(body, mesh=mesh, in_specs=in_specs, out_specs=out_specs, check_vma=False)
```

```python
import math

import jax
import jax.numpy as jnp
import numpy as np
from jax import lax
from jax.experimental import pallas as pl
from jax.experimental.pallas import tpu as pltpu
from jax.sharding import PartitionSpec as P

SIZE = 256
HALF = 128
MODES = 4
CHUNK = 16
SLOTS = 8
BF16 = jnp.bfloat16
F32 = jnp.float32


def dft_tables():
    index = np.arange(SIZE)
    phase = 2.0 * np.pi * ((index[:, None] * index[None, :]) % SIZE) / SIZE
    real = np.cos(phase) / math.sqrt(SIZE)
    imag = -np.sin(phase) / math.sqrt(SIZE)
    halves = []
    for first in range(2):
        re, im = real[first::2, :HALF], imag[first::2, :HALF]
        halves.append(np.block([[re, -im], [im, re]]))
    both = np.stack(halves + [half.T for half in halves])
    return jnp.asarray(both, F32).astype(BF16)


def sorter():
    index = np.arange(SIZE)
    place = index // 2 + HALF * (index % 2)
    sort = place[:, None] == index[None, :]
    return jnp.asarray(np.stack([sort, sort.T]), BF16)


def describe_kernel(info, notes):
    tiles = notes.shape[0]
    scans = (info.shape[0] - 2) // 4
    level = [(info[2 * n] // HALF) % 4 for n in range(scans)]
    straddles = [(info[2 * n + 1] // HALF) % 2 for n in range(scans)]
    tile = [info[2 * scans + 2 * n] for n in range(scans)]
    live = [(n < info[4 * scans]).astype(jnp.int32) for n in range(scans)]
    zero = jnp.int32(0)
    before, after = [zero] * scans, [zero] * scans
    for two in range(scans):
        for one in range(two):
            same = (tile[one] == tile[two]) & (straddles[one] + straddles[two] == 2)
            same = same.astype(jnp.int32)
            before[two], after[one] = before[two] | same, after[one] | same
    odd = info[4 * scans + 1]
    shift = [straddles[n] * jnp.where(odd == 1, 1 - after[n], before[n]) for n in range(scans)]
    owner = [tile[n] + shift[n] for n in range(scans)]
    aside = [jnp.where(straddles[n] == 1, 1 - shift[n], 2 * odd - 1) for n in range(scans)]
    other = [lax.rem(tile[n] + aside[n] + tiles, tiles) for n in range(scans)]
    for n in range(scans):
        free = live[n] * (1 - before[n]) * (1 - after[n])
        for k in range(scans):
            if k != n:
                free = free * (1 - (owner[k] == other[n]).astype(jnp.int32))
            if k < n:
                free = free * (1 - (other[k] == other[n]).astype(jnp.int32))
        column = (jnp.where(straddles[n] == 1, 2 - 2 * shift[n], 1) + odd) & 3
        moved_column = (jnp.where(straddles[n] == 1, 2 * shift[n], 3) + odd) & 3
        note = live[n] + 2 * free + 4 * owner[n] + 64 * other[n] + 1024 * level[n]
        note = note + 4096 * column + 16384 * moved_column
        for t in range(tiles):
            notes[t, 0, n] = note
    for t in range(tiles):
        for n in range(scans, SLOTS):
            notes[t, 0, n] = 0


def assign_kernel(me, notes, packed, codes, slots, loads, homes, sems):
    tiles = codes.shape[0]
    scans = packed.shape[0]
    for t in range(tiles):
        loads[t] = 0

    @pl.loop(0, tiles)
    def _(source):
        for n in range(scans):
            note = notes[source, 0, n]
            loads[(note >> 2) & 15] += note & 1

    @pl.loop(0, tiles)
    def _(source):
        code = jnp.int32(0)
        for n in range(scans):
            note = notes[source, 0, n]
            owner, other = (note >> 2) & 15, (note >> 6) & 15
            here, there = loads[owner], loads[other]
            move = ((note >> 1) & 1) * (here > there + 1).astype(jnp.int32)
            loads[owner] = here - move
            loads[other] = loads[other] + move
            home = jnp.where(move == 1, other, owner)
            column = (note >> (12 + 2 * move)) & 3
            mine = (note & 1) * (home == me[0]).astype(jnp.int32)
            code = code + mine * (1 + 4 * ((note >> 10) & 3) + column)

            @pl.when(source == me[0])
            def _():
                homes[n] = jnp.where((note & 1) == 1, home, -1)

        codes[source] = code

    def each(act):
        for n in range(scans):

            @pl.when(homes[n] >= 0)
            def _():
                act(pltpu.make_async_copy(packed.at[n], slots.at[homes[n]], sems.at[n]))

    each(lambda copy: copy.start())
    each(lambda copy: copy.wait())


def cast_kernel(odd, obj, tile_low, half):
    side = pl.multiple_of((1 - odd[0]) * HALF, HALF)
    tile_low[...] = obj[...].astype(BF16)
    half[...] = obj[:, :, :, pl.ds(side, HALF)].astype(BF16)


def sort_kernel(info, measured, sort, packed):
    scans = measured.shape[0]
    for n in range(scans):

        @pl.when(n < info[4 * scans])
        def _():
            rows = jnp.dot(sort[1], measured[n].astype(BF16), preferred_element_type=F32)
            both = jnp.dot(rows.astype(BF16), sort[0], preferred_element_type=F32)
            packed[n] = both.astype(BF16)


def banded(taps, row, shift):
    line = jnp.broadcast_to(taps[row : row + 1, :], (SIZE, 2 * SIZE))
    return pltpu.roll(line, shift, 1, stride=1, stride_axis=0)[:, :SIZE]


STRAIGHT, TURNED = 2 * SIZE - 32, 2 * SIZE - 31


def put_table(out, real, imag, from_left):
    sign = 1.0 if from_left else -1.0
    out[:SIZE, :SIZE] = real.astype(BF16)
    out[:SIZE, SIZE:] = (-sign * imag).astype(BF16)
    out[SIZE:, :SIZE] = (sign * imag).astype(BF16)
    out[SIZE:, SIZE:] = real.astype(BF16)


def put_tables(taps, tables):
    put_table(tables.at[0], banded(taps, 0, STRAIGHT), banded(taps, 1, STRAIGHT), True)
    put_table(tables.at[1], banded(taps, 6, TURNED), banded(taps, 7, TURNED), False)


def put_adjoints(taps, tables):
    put_table(tables.at[0], banded(taps, 4, TURNED), -banded(taps, 5, TURNED), True)
    put_table(tables.at[1], banded(taps, 2, STRAIGHT), -banded(taps, 3, STRAIGHT), False)


CHUNKS = [slice(at, at + CHUNK) for at in range(0, SIZE, CHUNK)]


def in_turn(*stages):
    for step in range(MODES + len(stages) - 1):
        for place, stage in enumerate(stages):
            if 0 <= step - place < MODES:
                stage(step - place)


def rows_of(m):
    return slice(m * SIZE, (m + 1) * SIZE)


def left_stage(table, rows_in, cols_in):
    def stage(m):
        both = jnp.dot(table, rows_in[m], preferred_element_type=F32)
        cols_in[rows_of(m), :SIZE] = both[:SIZE].astype(BF16)
        cols_in[rows_of(m), SIZE:] = both[SIZE:].astype(BF16)

    return stage


def right_stage(table, cols_in, out):
    def stage(m):
        out[rows_of(m), :] = jnp.dot(cols_in[rows_of(m), :], table, preferred_element_type=F32)

    return stage


def put_rows(rows_in, m, at, real, imag):
    rows_in[m, at.start : at.stop, :] = real.astype(BF16)
    rows_in[m, SIZE + at.start : SIZE + at.stop, :] = imag.astype(BF16)


def put_halves(rows_in, m, at, first, second):
    for place, part in enumerate(first + second):
        low = place * HALF + at.start
        rows_in[m, low : low + CHUNK, :] = part.astype(BF16)


def dft_left(dft, rows_in, cols_in):
    def stage(m):
        for first in range(2):
            part = slice(first * SIZE, (first + 1) * SIZE)
            both = jnp.dot(dft[first], rows_in[m, part, :], preferred_element_type=F32)
            rows = slice(m * SIZE + first * HALF, m * SIZE + (first + 1) * HALF)
            for k in range(2):
                here = both[k * HALF : (k + 1) * HALF]
                low, high = here[:, :HALF], here[:, HALF:]
                cols_in[rows, k * HALF : (k + 1) * HALF] = (low + high).astype(BF16)
                cols_in[rows, SIZE + k * HALF : SIZE + (k + 1) * HALF] = (low - high).astype(BF16)

    return stage


def dft_right(dft, cols_in, out):
    def stage(m):
        for first in range(2):
            part = slice(first * SIZE, (first + 1) * SIZE)
            both = jnp.dot(cols_in[rows_of(m), part], dft[2 + first], preferred_element_type=F32)
            for k in range(2):
                low = k * SIZE + first * HALF
                out[rows_of(m), low : low + HALF] = both[:, k * HALF : (k + 1) * HALF]

    return stage


def inverse_left(dft, rows_in, cols_in):
    def stage(m):
        even = jnp.dot(dft[2], rows_in[m, :SIZE, :], preferred_element_type=F32)
        odd = jnp.dot(dft[3], rows_in[m, SIZE:, :], preferred_element_type=F32)
        for k in range(2):
            part = slice(k * HALF, (k + 1) * HALF)
            sums = (even[part] + odd[part]).astype(BF16)
            gaps = (even[part] - odd[part]).astype(BF16)
            for side in range(2):
                here = slice(side * HALF, (side + 1) * HALF)
                low = side * SIZE + k * HALF
                cols_in[m * SIZE : m * SIZE + HALF, low : low + HALF] = sums[:, here]
                cols_in[m * SIZE + HALF : (m + 1) * SIZE, low : low + HALF] = gaps[:, here]

    return stage


def inverse_right(dft, cols_in, out):
    def stage(m):
        even = jnp.dot(cols_in[rows_of(m), :SIZE], dft[0], preferred_element_type=F32)
        odd = jnp.dot(cols_in[rows_of(m), SIZE:], dft[1], preferred_element_type=F32)
        for k in range(2):
            part = slice(k * HALF, (k + 1) * HALF)
            out[rows_of(m), k * SIZE : k * SIZE + HALF] = even[:, part] + odd[:, part]
            out[rows_of(m), k * SIZE + HALF : (k + 1) * SIZE] = even[:, part] - odd[:, part]

    return stage


def pair(ref, m, at):
    here = slice(m * SIZE + at.start, m * SIZE + at.stop)
    return ref[here, :SIZE], ref[here, SIZE:]


def extend(odd, full, tile, half, ext):
    ext[4 * odd] = half[...]
    ext[1 + odd], ext[2 + odd] = tile[:, :, :, :HALF], tile[:, :, :, HALF:]
    ext[3 - 3 * odd], ext[4 - 3 * odd] = full[:, :, :, :HALF], full[:, :, :, HALF:]


def live_list(codes, order):
    def note(slot, found):
        live = codes[slot] > 0

        @pl.when(live)
        def _():
            order[found] = slot

        return found + live.astype(jnp.int32)

    return lax.fori_loop(0, codes.shape[0], note, jnp.int32(0))


def place_of(code):
    return (code - 1) % 4, pl.multiple_of(((code - 1) // 4) * HALF, HALF)


def pair_of(patch, s, at):
    return patch[s, at, :SIZE].astype(F32), patch[s, at, SIZE:].astype(F32)


def forward_kernel(
    odd, codes, full, tile, half, probe, taps, dft,
    moved_all, far_all, root_all, patch_all,
    ext, tables, rows_in, cols_in, moved_two, far_two, root_two, patch_two, order, sems,
):
    extend(odd[0], full, tile, half, ext)
    put_tables(taps, tables)
    found = live_list(codes, order)
    wholes = (root_all, moved_all, far_all, patch_all)
    buffers = (root_two, moved_two, far_two, patch_two)

    def copies(i):
        two = lax.rem(i, 2)
        return [
            pltpu.make_async_copy(buffers[k].at[two], wholes[k].at[order[i]], sems.at[two, k])
            for k in range(4)
        ]

    @pl.loop(0, found)
    def _(i):
        two = lax.rem(i, 2)
        root, moved, far, patch = (buffer.at[two] for buffer in buffers)

        @pl.when(i >= 2)
        def _():
            for copy in copies(i - 2):
                copy.wait()

        column, start = place_of(codes[order[i]])
        for s in range(2):
            for part in range(2):
                for side in range(2):
                    low = part * SIZE + side * HALF
                    patch[s, :, low : low + HALF] = ext[column + side, s, part, pl.ds(start, SIZE), :]

        def wave(m):
            for at in CHUNKS:
                o_re, o_im = pair_of(patch, 0, at)
                p_re, p_im = probe[m, 0, at, :].astype(F32), probe[m, 1, at, :].astype(F32)
                put_rows(rows_in, m, at, p_re * o_re - p_im * o_im, p_re * o_im + p_im * o_re)

        def exit_wave(m):
            for at in CHUNKS[: len(CHUNKS) // 2]:
                down = slice(at.start + HALF, at.stop + HALF)
                o_re, o_im = pair_of(patch, 1, at)
                q_re, q_im = pair_of(patch, 1, down)
                v_re, v_im = pair(moved, m, at)
                w_re, w_im = pair(moved, m, down)
                a_re, a_im = v_re * o_re - v_im * o_im, v_re * o_im + v_im * o_re
                b_re, b_im = w_re * q_re - w_im * q_im, w_re * q_im + w_im * q_re
                put_halves(rows_in, m, at, (a_re + b_re, a_im + b_im), (a_re - b_re, a_im - b_im))

        in_turn(
            wave,
            left_stage(tables[0], rows_in, cols_in),
            right_stage(tables[1], cols_in, moved),
            exit_wave,
            dft_left(dft, rows_in, cols_in),
            dft_right(dft, cols_in, far),
        )
        for copy in copies(i)[1:]:
            copy.start()
        for at in CHUNKS:
            power = jnp.ones((CHUNK, SIZE), F32)
            for m in range(MODES):
                f_re, f_im = pair(far, m, at)
                power = power + (f_re * f_re + f_im * f_im)
            root[at, :] = 1.0 / jnp.sqrt(power)
        copies(i)[0].start()

    for last in (2, 1):

        @pl.when(found >= last)
        def _():
            for copy in copies(found - last):
                copy.wait()


def backward_kernel(
    odd, codes, dft, taps, probe_all,
    moved_all, far_all, root_all, patch_all, slots_all,
    own_grad, full_grad, half_grad, keep, give,
    rows_in, cols_in, moved_two, far_two, root_two, patch_two, slots_two,
    factor, probe, adjoints, acc, probe_acc, order, sems, once, ends,
):
    found = live_list(codes, order)
    wholes = (far_all, slots_all, root_all, moved_all, patch_all)
    buffers = (far_two, slots_two, root_two, moved_two, patch_two)
    probe_copy = pltpu.make_async_copy(probe_all, probe, once)

    def copies(i):
        two = lax.rem(i, 2)
        return [
            pltpu.make_async_copy(wholes[k].at[order[i]], buffers[k].at[two], sems.at[two, k])
            for k in range(5)
        ]

    @pl.when(found > 0)
    def _():
        for copy in copies(0) + [probe_copy]:
            copy.start()

    put_adjoints(taps, adjoints)
    acc[...] = jnp.zeros(acc.shape, F32)
    probe_acc[...] = jnp.zeros(probe_acc.shape, F32)

    def add_piece(s, at, column, start, g_re, g_im):
        rows = pl.ds(pl.multiple_of(start + at.start, CHUNK), CHUNK)
        for part, value in ((0, g_re), (1, g_im)):
            value = value.astype(BF16).astype(F32)
            for side in range(2):
                acc[column + side, s, part, rows, :] += value[:, side * HALF : (side + 1) * HALF]

    @pl.loop(0, found)
    def _(i):
        two = lax.rem(i, 2)
        far, slot, root, moved, patch = (buffer.at[two] for buffer in buffers)

        @pl.when(i + 1 < found)
        def _():
            for copy in copies(i + 1):
                copy.start()

        column, start = place_of(codes[order[i]])
        for copy in copies(i)[:3]:
            copy.wait()

        def scaled(m):
            for at in CHUNKS[: len(CHUNKS) // 2]:
                down = slice(at.start + HALF, at.stop + HALF)
                f_re, f_im = pair(far, m, at)
                g_re, g_im = pair(far, m, down)
                top, low = factor[at, :], factor[down, :]
                put_halves(rows_in, m, at, (top * f_re, top * f_im), (low * g_re, low * g_im))

        for at in CHUNKS:
            factor[at, :] = 1.0 - slot[at, :].astype(F32) * root[at, :]
        in_turn(
            scaled,
            inverse_left(dft, rows_in, cols_in),
            inverse_right(dft, cols_in, far),
        )
        for copy in copies(i)[3:]:
            copy.wait()
        for at in CHUNKS:
            o_re, o_im = pair_of(patch, 1, at)
            g_re = jnp.zeros((CHUNK, SIZE), F32)
            g_im = jnp.zeros((CHUNK, SIZE), F32)
            for m in range(MODES):
                a_re, a_im = pair(far, m, at)
                v_re, v_im = pair(moved, m, at)
                g_re = g_re + (v_re * a_re + v_im * a_im)
                g_im = g_im + (v_re * a_im - v_im * a_re)
                put_rows(rows_in, m, at, o_re * a_re + o_im * a_im, o_re * a_im - o_im * a_re)
            add_piece(1, at, column, start, g_re, g_im)

        in_turn(
            left_stage(adjoints[0], rows_in, cols_in),
            right_stage(adjoints[1], cols_in, moved),
        )

        @pl.when(i == 0)
        def _():
            probe_copy.wait()

        for at in CHUNKS:
            o_re, o_im = pair_of(patch, 0, at)
            g_re = jnp.zeros((CHUNK, SIZE), F32)
            g_im = jnp.zeros((CHUNK, SIZE), F32)
            for m in range(MODES):
                i_re, i_im = pair(moved, m, at)
                p_re, p_im = probe[m, 0, at, :].astype(F32), probe[m, 1, at, :].astype(F32)
                g_re = g_re + (p_re * i_re + p_im * i_im)
                g_im = g_im + (p_re * i_im - p_im * i_re)
                probe_acc[m, 0, at, :] += o_re * i_re + o_im * i_im
                probe_acc[m, 1, at, :] += o_re * i_im - o_im * i_re
            add_piece(0, at, column, start, g_re, g_im)

    leave = [
        pltpu.make_async_copy(
            acc.at[1 + side + odd[0]],
            own_grad.at[:, :, :, pl.ds(side * HALF, HALF)],
            ends.at[side],
        )
        for side in range(2)
    ]
    for copy in leave:
        copy.start()
    half_grad[...] = acc[4 * odd[0]].astype(BF16)
    full_grad[:, :, :, :HALF] = acc[3 - 3 * odd[0]].astype(BF16)
    full_grad[:, :, :, HALF:] = acc[4 - 3 * odd[0]].astype(BF16)
    modes = MODES // 2
    keep[...] = probe_acc[pl.ds(modes * odd[0], modes)].astype(BF16)
    give[...] = probe_acc[pl.ds(modes * (1 - odd[0]), modes)].astype(BF16)
    for copy in leave:
        copy.wait()


def whole(count):
    return [pl.BlockSpec(memory_space=pltpu.VMEM) for _ in range(count)]


def scalars(count):
    return [pl.BlockSpec(memory_space=pltpu.SMEM) for _ in range(count)]


def body(object_slices, probe, measured, tap_row, tap_col, scan_corner, correlation, scan_count):
    cols = lax.axis_size("col")
    rows = lax.axis_size("row")
    band = object_slices.shape[2]
    part_shape = (2, 2, band, HALF)
    limit = pltpu.CompilerParams(vmem_limit_bytes=56 * 1024 * 1024)

    tile_shape = (2, 2, band, SIZE)
    scans = measured.shape[0]
    odd = (lax.axis_index("row") % 2).reshape(1)
    def anywhere(count):
        return [pl.BlockSpec(memory_space=pl.ANY) for _ in range(count)]

    def ring(step):
        pairs = []
        for r in range(rows):
            way = step if r % 2 == 0 else -step
            pairs += [(r * cols + c, r * cols + (c + way) % cols) for c in range(cols)]
        return pairs

    both = ("row", "col")
    tile_low, half = pl.pallas_call(
        cast_kernel,
        out_shape=[
            jax.ShapeDtypeStruct(tile_shape, BF16),
            jax.ShapeDtypeStruct(part_shape, BF16),
        ],
        in_specs=scalars(1) + whole(1),
        out_specs=whole(2),
        compiler_params=limit,
    )(odd, object_slices)
    full = lax.ppermute(tile_low, both, ring(-1))
    half = lax.ppermute(half, both, ring(1))

    info = [scan_corner.reshape(-1), correlation.reshape(-1), scan_count.reshape(-1), odd]
    info = jnp.concatenate(info)
    notes = pl.pallas_call(
        describe_kernel,
        out_shape=jax.ShapeDtypeStruct((cols, 1, SLOTS), jnp.int32),
        in_specs=scalars(1),
        out_specs=pl.BlockSpec(memory_space=pltpu.SMEM),
        compiler_params=limit,
    )(info)
    row_notes = lax.all_to_all(notes, "col", split_axis=0, concat_axis=0, tiled=True)
    packed = pl.pallas_call(
        sort_kernel,
        out_shape=jax.ShapeDtypeStruct((scans, SIZE, SIZE), BF16),
        in_specs=scalars(1) + whole(2),
        out_specs=pl.BlockSpec(memory_space=pltpu.VMEM),
        compiler_params=limit,
    )(info, measured, sorter())
    codes, slots = pl.pallas_call(
        assign_kernel,
        out_shape=[
            jax.ShapeDtypeStruct((cols,), jnp.int32),
            jax.ShapeDtypeStruct((cols, SIZE, SIZE), BF16),
        ],
        in_specs=scalars(2) + whole(1),
        out_specs=scalars(1) + anywhere(1),
        scratch_shapes=[
            pltpu.SMEM((cols,), jnp.int32),
            pltpu.SMEM((scans,), jnp.int32),
            pltpu.SemaphoreType.DMA((scans,)),
        ],
        compiler_params=limit,
    )(lax.axis_index("col").reshape(1), row_notes, packed)
    arrived = lax.all_to_all(slots, "col", split_axis=0, concat_axis=0, tiled=True)

    taps = jnp.concatenate([tap_row, tap_col], axis=0)
    taps = jnp.concatenate([taps, taps[:, ::-1]], axis=0)
    taps = jnp.pad(taps, ((0, 0), (0, 2 * SIZE - taps.shape[1])))
    dft = dft_tables()

    field_shape = (MODES * SIZE, 2 * SIZE)
    patch_shape = (2, SIZE, 2 * SIZE)
    pair_shape = (2, 2 * SIZE, 2 * SIZE)
    work = [
        pltpu.VMEM((MODES, 2 * SIZE, SIZE), BF16),
        pltpu.VMEM(field_shape, BF16),
        pltpu.VMEM((2,) + field_shape, F32),
        pltpu.VMEM((2,) + field_shape, F32),
        pltpu.VMEM((2, SIZE, SIZE), F32),
        pltpu.VMEM((2,) + patch_shape, BF16),
    ]
    order = pltpu.SMEM((cols,), jnp.int32)
    moved_all, far_all, root_all, patch_all = pl.pallas_call(
        forward_kernel,
        out_shape=[
            jax.ShapeDtypeStruct((cols,) + field_shape, F32),
            jax.ShapeDtypeStruct((cols,) + field_shape, F32),
            jax.ShapeDtypeStruct((cols, SIZE, SIZE), F32),
            jax.ShapeDtypeStruct((cols,) + patch_shape, BF16),
        ],
        in_specs=scalars(2) + whole(6),
        out_specs=anywhere(4),
        scratch_shapes=[pltpu.VMEM((5,) + part_shape, BF16), pltpu.VMEM(pair_shape, BF16)]
        + work
        + [order, pltpu.SemaphoreType.DMA((2, 4))],
        cost_estimate=pl.CostEstimate(flops=40 * 10**9, bytes_accessed=10**7, transcendentals=0),
        compiler_params=limit,
    )(odd, codes, full, tile_low, half, probe, taps, dft)
    half_probe = (MODES // 2,) + probe.shape[1:]
    own_grad, full_grad, half_grad, keep, give = pl.pallas_call(
        backward_kernel,
        out_shape=[
            jax.ShapeDtypeStruct(tile_shape, F32),
            jax.ShapeDtypeStruct(tile_shape, BF16),
            jax.ShapeDtypeStruct(part_shape, BF16),
            jax.ShapeDtypeStruct(half_probe, BF16),
            jax.ShapeDtypeStruct(half_probe, BF16),
        ],
        in_specs=scalars(2) + whole(2) + anywhere(6),
        out_specs=anywhere(1) + whole(4),
        scratch_shapes=work
        + [
            pltpu.VMEM((2, SIZE, SIZE), BF16),
            pltpu.VMEM((SIZE, SIZE), F32),
            pltpu.VMEM(probe.shape, BF16),
            pltpu.VMEM(pair_shape, BF16),
            pltpu.VMEM((5,) + part_shape, F32),
            pltpu.VMEM(probe.shape, F32),
            order,
            pltpu.SemaphoreType.DMA((2, 5)),
            pltpu.SemaphoreType.DMA,
            pltpu.SemaphoreType.DMA((2,)),
        ],
        compiler_params=limit,
    )(
        odd, codes, dft, taps, probe,
        moved_all, far_all, root_all, patch_all, arrived,
    )

    share = MODES * SIZE // cols
    partner = [(r * cols + c, (r ^ 1) * cols + c) for r in range(rows) for c in range(cols)]

    def swap(blocks, axis):
        return lax.all_to_all(blocks, axis, split_axis=0, concat_axis=0, tiled=True)

    given = lax.ppermute(give, both, partner)
    mine = (keep.astype(F32) + given.astype(F32)).astype(BF16)
    mine = swap(mine.reshape(cols, share, SIZE), "col")
    mine = jnp.sum(mine.astype(F32), axis=0).astype(BF16)
    mine, full_grad, half_grad = lax.optimization_barrier((mine, full_grad, half_grad))
    full_grad = lax.ppermute(full_grad, both, ring(1))
    half_grad = lax.ppermute(half_grad, both, ring(-1))
    mine = swap(jnp.broadcast_to(mine[None], (rows, share, SIZE)), "row")
    same = (jnp.arange(rows) % 2 == odd[0]).astype(F32)
    scale = 1.0 / math.sqrt(scans * cols * rows)
    mine = (jnp.sum(mine.astype(F32) * same[:, None, None], axis=0) * scale).astype(BF16)
    mine, full_grad = lax.optimization_barrier((mine, full_grad))
    mine = swap(jnp.broadcast_to(mine[None], (cols, share, SIZE)), "col").reshape(half_probe)
    mine, half_grad = lax.optimization_barrier((mine, half_grad))
    given = lax.ppermute(mine, both, partner)
    even = odd[0] == 0
    probe_grad = [jnp.where(even, mine, given), jnp.where(even, given, mine)]
    probe_grad = jnp.concatenate(probe_grad, axis=0).astype(F32)
    half_grad = half_grad.astype(F32)
    nothing = jnp.zeros_like(half_grad)
    odd = odd[0] == 1
    halo = [jnp.where(odd, half_grad, nothing), jnp.where(odd, nothing, half_grad)]
    return own_grad + full_grad.astype(F32) + jnp.concatenate(halo, axis=-1), probe_grad


def solution(mesh):
    in_specs = (
        P(None, None, "row", "col"),
        P(),
        P(("row", "col"), None, None),
        P(),
        P(),
        P(("row", "col"), None),
        P(("row", "col"), None),
        P("row", "col"),
    )
    out_specs = (P(None, None, "row", "col"), P())
    return jax.shard_map(body, mesh=mesh, in_specs=in_specs, out_specs=out_specs, check_vma=False)
```
